32 devices in a mesh: ctx: 8 (over z, y), wsh: 4 (over x, core).
Axes of the slice: x: 2, y: 2, z: 4, core: 2. Of those that a mesh axis runs over, the one named last changes fastest.
Arguments:
- inputs: bfloat16 [8, 2, 1024, 960], P('wsh', None, 'ctx'), may hold values from -6 to 6
- norm1_gain: bfloat16 [960], P('wsh'), may hold values from 0.25 to 1.75
- q_weight: bfloat16 [960, 960], P('wsh'), may hold values from -0.1875 to 0.1875
- k_weight: bfloat16 [960, 320], P('wsh'), may hold values from -0.1875 to 0.1875
- v_weight: bfloat16 [960, 320], P('wsh'), may hold values from -0.1875 to 0.1875
- o_weight: bfloat16 [960, 960], P('wsh'), may hold values from -1 to 1
- norm2_gain: bfloat16 [960], P('wsh'), may hold values from 0.25 to 1.75
- gate_weight: bfloat16 [960, 2560], P('wsh'), may hold values from -0.1875 to 0.1875
- up_weight: bfloat16 [960, 2560], P('wsh'), may hold values from -0.1875 to 0.1875
- down_weight: bfloat16 [2560, 960], P('wsh'), may hold values from -0.125 to 0.125
- cotangent: bfloat16 [8, 2, 1024, 960], P('wsh', None, 'ctx'), may hold values from -6 to 6
Outputs:
- output: bfloat16 [8, 2, 1024, 960], P('wsh', None, 'ctx')
- input_grad: float32 [8, 2, 1024, 960], P('wsh', None, 'ctx')
- norm1_gain_grad: float32 [960], P('wsh')
- q_weight_grad: float32 [960, 960], P('wsh')
- k_weight_grad: float32 [960, 320], P('wsh')
- v_weight_grad: float32 [960, 320], P('wsh')
- o_weight_grad: float32 [960, 960], P('wsh')
- norm2_gain_grad: float32 [960], P('wsh')
- gate_weight_grad: float32 [960, 2560], P('wsh')
- up_weight_grad: float32 [960, 2560], P('wsh')
- down_weight_grad: float32 [2560, 960], P('wsh')
The draws below stay inside these ranges and needn't reach their ends.
All inputs are finite; a program needn't handle non-finite values.
Results may differ from the reference program's by a relative error of at most 0.022.
Values may be sent and summed in bfloat16 or wider, within the bound.
No kernel may reach another device: no remote copies, remote signals or barrier semaphores. Data moves between devices by JAX's collectives and lax.ppermute only.
A program may use at most 256 MiB of HBM per device.

```python
import math
import jax
import jax.numpy as jnp
from jax import lax

D = 960
FF = 2560
HEADS = 15
KV_HEADS = 5
HEAD = 64
BLK = 128
HALF = 1024
SEQS = 8
N_CTX = 8


def shard_levels(key, dims, cuts, smallest, largest):
    factor_of = 1.0
    for axis_at, shards_of in cuts:
        heights = jax.random.uniform(jax.random.fold_in(jax.random.fold_in(key, 6), axis_at), (shards_of,), jnp.float32, smallest / len(cuts), largest / len(cuts))
        factor_of = factor_of * jnp.repeat(jnp.exp(heights), dims[axis_at] // shards_of).reshape((-1,) + (1,) * (len(dims) - 1 - axis_at))
    return factor_of


def normal_values(own_key, shape, scale, limit, cuts=(), kind=jnp.bfloat16):
    array = scale * jax.random.normal(own_key, shape, jnp.float32)
    if cuts:
        array = array * shard_levels(own_key, shape, cuts, -0.22, 0.18)
    return jnp.clip(array, -limit, limit).astype(kind)


def setup_inputs(seed: int = 0) -> dict:
    arg_keys = jax.random.split(jax.random.key(seed), 12)
    inputs = normal_values(arg_keys[0], (SEQS, 2, HALF, D), 1.0, 6.0, ((0, 4), (2, 8)))
    norm1_gain = jnp.clip(1.0 + 0.15 * jax.random.normal(arg_keys[1], (D,), jnp.float32), 0.25, 1.75).astype(jnp.bfloat16)
    q_weight = normal_values(arg_keys[2], (D, HEADS * HEAD), D ** -0.5, 0.1875, ((0, 4),))
    k_weight = normal_values(arg_keys[3], (D, KV_HEADS * HEAD), D ** -0.5, 0.1875, ((0, 4),))
    v_weight = normal_values(arg_keys[4], (D, KV_HEADS * HEAD), D ** -0.5, 0.1875, ((0, 4),))
    o_weight = normal_values(arg_keys[5], (HEADS * HEAD, D), (HEADS * HEAD // 32) ** -0.5, 1.0, ((0, 4),))
    norm2_gain = jnp.clip(1.0 + 0.15 * jax.random.normal(arg_keys[6], (D,), jnp.float32), 0.25, 1.75).astype(jnp.bfloat16)
    gate_weight = normal_values(arg_keys[7], (D, FF), D ** -0.5, 0.1875, ((0, 4),))
    up_weight = normal_values(arg_keys[8], (D, FF), D ** -0.5, 0.1875, ((0, 4),))
    down_weight = normal_values(arg_keys[9], (FF, D), FF ** -0.5, 0.125, ((0, 4),))
    cotangent = normal_values(arg_keys[10], (SEQS, 2, HALF, D), 1.0, 6.0, ((0, 4), (2, 8)))
    return dict(inputs=inputs, norm1_gain=norm1_gain, q_weight=q_weight, k_weight=k_weight, v_weight=v_weight, o_weight=o_weight, norm2_gain=norm2_gain, gate_weight=gate_weight, up_weight=up_weight, down_weight=down_weight, cotangent=cotangent)


EPSILON = 1e-05
MASKED = -1e+30
HIGHEST_PRECISION = lax.Precision.HIGHEST

@jax.custom_vjp
def low(v):
    return lax.optimization_barrier(v.astype(jnp.bfloat16)).astype(jnp.float32)

@jax.custom_vjp
def low_back(v):
    return v

def low_keep(v):
    return (low(v), None)

def low_pass(kept, grad):
    return (grad,)

def back_keep(v):
    return (v, None)

def back_low(kept, grad):
    return (low(grad),)
low.defvjp(low_keep, low_pass)
low_back.defvjp(back_keep, back_low)

def rotary(values, places, direction):
    half_size = values.shape[-1] // 2
    frequency = jnp.exp(jnp.arange(half_size).astype(jnp.float32) * (-math.log(10000.0) / half_size))
    angles = places[:, None] * frequency[None, :]
    cosine = jnp.cos(angles)[:, None, :]
    sine = direction * jnp.sin(angles)[:, None, :]
    first_half = values[..., :half_size]
    second_half = values[..., half_size:]
    return jnp.concatenate([first_half * cosine - second_half * sine, second_half * cosine + first_half * sine], -1)

def rms_scale(stream):
    return lax.rsqrt(lax.optimization_barrier(jnp.mean(stream * stream, -1, keepdims=True)) + EPSILON)

def matmul(left, right):
    return jnp.dot(left, right, precision=HIGHEST_PRECISION)

def mirrored_to_plain(arrays):
    seq_count = arrays.shape[0]
    model_width = arrays.shape[-1]
    front = arrays[:, 0]
    back = arrays[:, 1].reshape(seq_count, N_CTX, BLK, model_width)[:, ::-1].reshape(seq_count, N_CTX * BLK, model_width)
    return jnp.concatenate([front, back], 1)

def plain_to_mirrored(arrays):
    seq_count = arrays.shape[0]
    model_width = arrays.shape[-1]
    half_len = arrays.shape[1] // 2
    front = arrays[:, :half_len]
    back = arrays[:, half_len:].reshape(seq_count, N_CTX, BLK, model_width)[:, ::-1].reshape(seq_count, half_len, model_width)
    return jnp.stack([front, back], 1)

def attention(queries, key_rows, value_rows):
    length = queries.shape[0]
    groups = HEADS // KV_HEADS
    score_scale = HEAD ** (-0.5)
    query_heads = queries.reshape(length, KV_HEADS, groups, HEAD)
    key_heads = key_rows.reshape(length, KV_HEADS, HEAD)
    value_heads = value_rows.reshape(length, KV_HEADS, HEAD)
    block_rows = math.gcd(length, 512)
    key_places = jnp.arange(length, dtype=jnp.int32)

    def one_block(block_index):
        query_block = lax.dynamic_slice_in_dim(query_heads, block_index * block_rows, block_rows, 0)
        raw_scores = jnp.einsum('qhgd,khd->hgqk', query_block, key_heads, precision=HIGHEST_PRECISION)
        scores = low_back(raw_scores) * score_scale
        query_places = block_index * block_rows + jnp.arange(block_rows, dtype=jnp.int32)
        allowed = key_places[None, :] <= query_places[:, None]
        scores = jnp.where(allowed, scores, MASKED)
        weights_f = jax.nn.softmax(scores, -1)
        return jnp.einsum('hgqk,khd->qhgd', low(weights_f), value_heads, precision=HIGHEST_PRECISION)
    blocks_out = lax.map(jax.checkpoint(one_block), jnp.arange(length // block_rows, dtype=jnp.int32))
    return blocks_out.reshape(length, HEADS * HEAD)

def one_sequence(stream, gain_one, weight_q, weight_k, weight_v, weight_o, gain_two, weight_gate, weight_up, weight_down):
    length = stream.shape[0]
    places = jnp.arange(length).astype(jnp.float32)
    normed = low(stream * rms_scale(stream) * gain_one)
    queries = low(rotary(low_back(matmul(normed, weight_q)).reshape(length, HEADS, HEAD), places, 1.0).reshape(length, HEADS * HEAD))
    key_rows = low(rotary(low_back(matmul(normed, weight_k)).reshape(length, KV_HEADS, HEAD), places, 1.0).reshape(length, KV_HEADS * HEAD))
    value_rows = low(low_back(matmul(normed, weight_v)))
    attn_rows = low(low_back(attention(queries, key_rows, value_rows)))
    middle = stream + low_back(matmul(attn_rows, weight_o))
    normed_two = low(middle * rms_scale(middle) * gain_two)
    gate_pre = low_back(matmul(normed_two, weight_gate))
    up_pre = low_back(matmul(normed_two, weight_up))
    hidden = low(jax.nn.silu(gate_pre) * up_pre)
    return middle + matmul(hidden, weight_down)

def reference(inputs, norm1_gain, q_weight, k_weight, v_weight, o_weight, norm2_gain, gate_weight, up_weight, down_weight, cotangent):
    params = tuple((weight.astype(jnp.float32) for weight in (norm1_gain, q_weight, k_weight, v_weight, o_weight, norm2_gain, gate_weight, up_weight, down_weight)))
    plain_rows = mirrored_to_plain(inputs.astype(jnp.float32))

    def whole_layer(plain_in, gain_one, weight_q, weight_k, weight_v, weight_o, gain_two, weight_gate, weight_up, weight_down):

        def per_sequence(sequence):
            return one_sequence(sequence, gain_one, weight_q, weight_k, weight_v, weight_o, gain_two, weight_gate, weight_up, weight_down)
        return lax.map(per_sequence, plain_in)
    result, pullback = jax.vjp(whole_layer, plain_rows, *params)
    gradients = pullback(mirrored_to_plain(cotangent.astype(jnp.float32)))
    return (plain_to_mirrored(result).astype(jnp.bfloat16), plain_to_mirrored(gradients[0]), gradients[1], gradients[2], gradients[3], gradients[4], gradients[5], gradients[6], gradients[7], gradients[8], gradients[9])
```

```python
import functools
import math

import jax
import jax.numpy as jnp
from jax import lax
from jax.experimental import pallas as pl
from jax.experimental.pallas import tpu as pltpu
from jax.sharding import PartitionSpec as P

HEADS = 15
KV_HEADS = 5
HEAD = 64
GROUPS = HEADS // KV_HEADS
KV_WIDTH = KV_HEADS * HEAD
LANES = 128
EPSILON = 1e-05
MASKED = -1e30
SCALE = HEAD ** (-0.5)
VMEM_BYTES = 56 * 1024 * 1024

NT = (((1,), (1,)), ((), ()))
TN = (((0,), (0,)), ((), ()))


def dot(a, b, dims=None):
    if dims is None:
        return jnp.dot(a, b, preferred_element_type=jnp.float32)
    return lax.dot_general(a, b, dims, preferred_element_type=jnp.float32)


def lane_ids(shape):
    return lax.broadcasted_iota(jnp.int32, shape, 1)


def turn(u, cosine, sine):
    first = (lane_ids(u.shape) & 32) == 0
    partner = jnp.where(first, pltpu.roll(u, 96, 1), pltpu.roll(u, 32, 1))
    return u * cosine + partner * sine


def rope_tables(ctx_rank, ctx_count, block_len):
    offsets = jnp.arange(block_len, dtype=jnp.int32)
    front = ctx_rank * block_len + offsets
    back = (2 * ctx_count - 1 - ctx_rank) * block_len + offsets
    places = jnp.concatenate([front, back]).astype(jnp.float32)
    half = HEAD // 2
    frequency = jnp.exp(jnp.arange(half).astype(jnp.float32) * (-math.log(10000.0) / half))
    angles = places[:, None] * frequency[None, :]
    cosine = jnp.cos(angles)
    sine = jnp.sin(angles)
    return (
        jnp.concatenate([cosine] * 4, 1),
        jnp.concatenate([-sine, sine, -sine, sine], 1),
    )


def load_tile(ref, lead, tile, width):
    lo = tile * LANES
    hi = min(lo + LANES, width)
    value = ref[lead + (slice(None), slice(lo, hi))].astype(jnp.float32)
    if hi - lo < LANES:
        value = jnp.concatenate(
            [value, jnp.zeros((value.shape[0], LANES - (hi - lo)), jnp.float32)], 1
        )
    return value


def place_head(value, parity_from, parity_to):
    if parity_from != parity_to:
        value = pltpu.roll(value, HEAD, 1)
    keep = (lane_ids(value.shape) // HEAD) == parity_to
    return jnp.where(keep, value, 0.0)


def head_rows(ref, half, head, parity, width):
    parts = []
    for g in range(GROUPS):
        j = head * GROUPS + g
        parts.append(place_head(load_tile(ref, (0, half), j // 2, width), j % 2, parity))
    return jnp.concatenate(parts, 0)


def attend_kernel(n, block, rank_ref, q_ref, kv_ref, o_ref, lse_ref, qs, wide, narrow, top, total, acc):
    c = rank_ref[0]
    rows = GROUPS * block
    pair = 2 * block
    q_at = lax.broadcasted_iota(jnp.int32, (rows, block), 0) % block
    k_at = lax.broadcasted_iota(jnp.int32, (rows, block), 1)
    causal = k_at <= q_at
    unroll = n if n <= 8 else 4
    for h in range(KV_HEADS):
        kt, kp = h // 2, h % 2
        vt, vp = (KV_HEADS + h) // 2, (KV_HEADS + h) % 2
        kl, vl = pl.ds(kt * LANES, LANES), pl.ds(vt * LANES, LANES)
        for half in range(2):
            qs[half] = head_rows(q_ref, half, h, kp, q_ref.shape[-1]).astype(jnp.bfloat16)
        top[...] = jnp.full_like(top, MASKED)

        def wide_scores(i, carry):
            s = dot(qs[1], kv_ref[0, 0, pl.ds(i * pair, pair), kl], NT)
            wide[i] = s
            top[1] = jnp.maximum(top[1], jnp.maximum(s[:, :block], s[:, block:]))
            return carry

        lax.fori_loop(0, n // 2, wide_scores, 0, unroll=2)

        def narrow_scores(d, carry):
            sel = (d > c).astype(jnp.int32)
            s = dot(qs[sel], kv_ref[0, sel, pl.ds(d * block, block), kl], NT)
            s = jnp.where(jnp.logical_or(causal, d != c), s, MASKED)
            narrow[d] = s
            top[sel] = jnp.maximum(top[sel], s)
            return carry

        lax.fori_loop(0, n, narrow_scores, 0, unroll=unroll)
        s = dot(qs[1], kv_ref[0, 1, pl.ds(c * block, block), kl], NT)
        s = jnp.where(causal, s, MASKED)
        narrow[n] = s
        top[1] = jnp.maximum(top[1], s)
        for half in range(2):
            top[half] = jnp.broadcast_to(
                jnp.max(top[half], axis=1, keepdims=True), (rows, LANES)
            )
        total[...] = jnp.zeros_like(total)
        acc[...] = jnp.zeros_like(acc)

        def wide_sums(i, carry):
            t = top[1]
            s = wide[i]
            pa = jnp.exp(s[:, :block] - t)
            pb = jnp.exp(s[:, block:] - t)
            total[1] += pa + pb
            p = jnp.concatenate([pa, pb], 1).astype(jnp.bfloat16)
            acc[1] += dot(p, kv_ref[0, 0, pl.ds(i * pair, pair), vl])
            return carry

        lax.fori_loop(0, n // 2, wide_sums, 0, unroll=2)

        def narrow_sums(d, carry):
            sel = (d > c).astype(jnp.int32)
            p = jnp.exp(narrow[d] - top[sel])
            total[sel] += p
            acc[sel] += dot(p.astype(jnp.bfloat16), kv_ref[0, sel, pl.ds(d * block, block), vl])
            return carry

        lax.fori_loop(0, n, narrow_sums, 0, unroll=unroll)
        p = jnp.exp(narrow[n] - top[1])
        total[1] += p
        acc[1] += dot(p.astype(jnp.bfloat16), kv_ref[0, 1, pl.ds(c * block, block), vl])
        for half in range(2):
            whole = jnp.broadcast_to(jnp.sum(total[half], axis=1, keepdims=True), (rows, LANES))
            out = acc[half] / whole
            lse = top[half] + jnp.log(whole)
            lse_ref[0, 2 * h + half : 2 * h + half + 1, :] = lse.T[0:1, :]
            for g in range(GROUPS):
                j = h * GROUPS + g
                value = out[g * block : (g + 1) * block]
                if vp != j % 2:
                    value = pltpu.roll(value, HEAD, 1)
                lo = j * HEAD
                o_ref[0, half, :, lo : lo + HEAD] = value[:, (j % 2) * HEAD : (j % 2 + 1) * HEAD]


def attend(rank, queries, pairs, width):
    seqs, _, block, q_width = queries.shape
    n = pairs.shape[2] // block
    rows = GROUPS * block
    return pl.pallas_call(
        functools.partial(attend_kernel, n, block),
        grid=(seqs,),
        in_specs=[
            pl.BlockSpec(memory_space=pltpu.SMEM),
            pl.BlockSpec((1, 2, block, q_width), lambda b: (b, 0, 0, 0)),
            pl.BlockSpec((1, 2, n * block, 2 * KV_WIDTH), lambda b: (b, 0, 0, 0)),
        ],
        out_specs=[
            pl.BlockSpec((1, 2, block, width), lambda b: (b, 0, 0, 0)),
            pl.BlockSpec((1, 2 * KV_HEADS, rows), lambda b: (b, 0, 0)),
        ],
        out_shape=[
            jax.ShapeDtypeStruct((seqs, 2, block, width), jnp.float32),
            jax.ShapeDtypeStruct((seqs, 2 * KV_HEADS, rows), jnp.float32),
        ],
        scratch_shapes=[
            pltpu.VMEM((2, rows, LANES), jnp.bfloat16),
            pltpu.VMEM((n // 2, rows, 2 * block), jnp.float32),
            pltpu.VMEM((n + 1, rows, block), jnp.float32),
            pltpu.VMEM((2, rows, LANES), jnp.float32),
            pltpu.VMEM((2, rows, LANES), jnp.float32),
            pltpu.VMEM((2, rows, LANES), jnp.float32),
        ],
        compiler_params=pltpu.CompilerParams(vmem_limit_bytes=VMEM_BYTES),
        cost_estimate=pl.CostEstimate(
            flops=4 * seqs * HEADS * block * block * HEAD * (2 * n + 1),
            bytes_accessed=8 * 1024 * 1024,
            transcendentals=seqs * HEADS * block * block * (2 * n + 1),
        ),
        name="attend",
    )(rank, queries, pairs)


def attend_back_kernel(
    n, block, rank_ref, q_ref, kv_ref, do_ref, o_ref, lse_ref, cos_ref, sin_ref,
    dq_ref, dkv_ref, qs, dos, inner, dqt, dkv, dq_full,
):
    c = rank_ref[0]
    rows = GROUPS * block
    pair = 2 * block
    width = do_ref.shape[-1]
    k_at = lax.broadcasted_iota(jnp.int32, (block, rows), 0)
    q_at = lax.broadcasted_iota(jnp.int32, (block, rows), 1) % block
    causal = k_at <= q_at
    unroll = n if n <= 8 else 4
    dkv[...] = jnp.zeros_like(dkv)
    dq_full[...] = jnp.zeros_like(dq_full)
    for h in range(KV_HEADS):
        kt, kp = h // 2, h % 2
        vt, vp = (KV_HEADS + h) // 2, (KV_HEADS + h) % 2
        kl, vl = pl.ds(kt * LANES, LANES), pl.ds(vt * LANES, LANES)
        for half in range(2):
            qs[half] = head_rows(q_ref, half, h, kp, q_ref.shape[-1]).astype(jnp.bfloat16)
            inner_parts = []
            do_parts = []
            for g in range(GROUPS):
                j = h * GROUPS + g
                d_o = load_tile(do_ref, (0, half), j // 2, width)
                o = load_tile(o_ref, (0, half), j // 2, width)
                product = place_head(d_o * o, j % 2, j % 2)
                inner_parts.append(jnp.sum(product.T, axis=0, keepdims=True))
                do_parts.append(place_head(d_o, j % 2, vp))
            dos[half] = jnp.concatenate(do_parts, 0).astype(jnp.bfloat16)
            inner[half] = jnp.concatenate(inner_parts, 1)
        dqt[...] = jnp.zeros_like(dqt)

        def visit(sel, half, start, count, mask):
            keys = kv_ref[0, half, pl.ds(start, count), kl]
            values = kv_ref[0, half, pl.ds(start, count), vl]
            s = dot(keys, qs[sel], NT)
            p = jnp.exp(s - lse_ref[0, pl.ds(2 * h + sel, 1), :])
            if mask is not None:
                p = jnp.where(mask, p, 0.0)
            dp = dot(values, dos[sel], NT)
            ds = (p * (dp - inner[sel])).astype(jnp.bfloat16)
            dkv[half, pl.ds(start, count), kl] += dot(ds, qs[sel])
            dkv[half, pl.ds(start, count), vl] += dot(p.astype(jnp.bfloat16), dos[sel])
            dqt[sel] += dot(keys, ds, TN)

        def wide_visit(i, carry):
            visit(1, 0, i * pair, pair, None)
            return carry

        lax.fori_loop(0, n // 2, wide_visit, 0, unroll=2)

        def narrow_visit(d, carry):
            sel = (d > c).astype(jnp.int32)
            visit(sel, sel, d * block, block, jnp.logical_or(causal, d != c))
            return carry

        lax.fori_loop(0, n, narrow_visit, 0, unroll=unroll)
        visit(1, 1, c * block, block, causal)
        for half in range(2):
            grad = dqt[half].T * SCALE
            for g in range(GROUPS):
                j = h * GROUPS + g
                tile = pl.ds((j // 2) * LANES, LANES)
                dq_full[half, :, tile] += place_head(
                    grad[g * block : (g + 1) * block], kp, j % 2
                )
    for half in range(2):
        at = slice(half * block, (half + 1) * block)
        for t in range(dq_full.shape[-1] // LANES):
            value = turn(
                dq_full[half, :, t * LANES : (t + 1) * LANES], cos_ref[at], -sin_ref[at]
            ).astype(jnp.bfloat16)
            hi = min((t + 1) * LANES, width)
            dq_ref[0, half, :, t * LANES : hi] = value[:, : hi - t * LANES]
    dkv_ref[0] = dkv[...].astype(jnp.bfloat16)


def attend_back(rank, queries, pairs, grad_attn, attended, lse, cosine, sine):
    seqs, _, block, q_width = queries.shape
    width = grad_attn.shape[-1]
    n = pairs.shape[2] // block
    rows = GROUPS * block
    whole4 = lambda b: (b, 0, 0, 0)
    buffers = pl.Buffered(2 if n <= 8 else 1)
    return pl.pallas_call(
        functools.partial(attend_back_kernel, n, block),
        grid=(seqs,),
        in_specs=[
            pl.BlockSpec(memory_space=pltpu.SMEM),
            pl.BlockSpec((1, 2, block, q_width), whole4),
            pl.BlockSpec((1, 2, n * block, 2 * KV_WIDTH), whole4, pipeline_mode=buffers),
            pl.BlockSpec((1, 2, block, width), whole4),
            pl.BlockSpec((1, 2, block, width), whole4),
            pl.BlockSpec((1, 2 * KV_HEADS, rows), lambda b: (b, 0, 0)),
            pl.BlockSpec((2 * block, LANES), lambda b: (0, 0)),
            pl.BlockSpec((2 * block, LANES), lambda b: (0, 0)),
        ],
        out_specs=[
            pl.BlockSpec((1, 2, block, width), whole4),
            pl.BlockSpec((1, 2, n * block, 2 * KV_WIDTH), whole4, pipeline_mode=buffers),
        ],
        out_shape=[
            jax.ShapeDtypeStruct((seqs, 2, block, width), jnp.bfloat16),
            jax.ShapeDtypeStruct((seqs, 2, n * block, 2 * KV_WIDTH), jnp.bfloat16),
        ],
        scratch_shapes=[
            pltpu.VMEM((2, rows, LANES), jnp.bfloat16),
            pltpu.VMEM((2, rows, LANES), jnp.bfloat16),
            pltpu.VMEM((2, 1, rows), jnp.float32),
            pltpu.VMEM((2, LANES, rows), jnp.float32),
            pltpu.VMEM((2, n * block, 2 * KV_WIDTH), jnp.float32),
            pltpu.VMEM((2, block, q_width), jnp.float32),
        ],
        compiler_params=pltpu.CompilerParams(vmem_limit_bytes=VMEM_BYTES),
        cost_estimate=pl.CostEstimate(
            flops=10 * seqs * HEADS * block * block * HEAD * (2 * n + 1),
            bytes_accessed=16 * 1024 * 1024,
            transcendentals=seqs * HEADS * block * block * (2 * n + 1),
        ),
        name="attend_back",
    )(rank, queries, pairs, grad_attn, attended, lse, cosine, sine)


def pieces_of(shard, axis):
    count = lax.axis_size(axis)
    found = {0: shard}
    bit = count // 2
    while bit:
        swap = [(i, i ^ bit) for i in range(count)]
        for p in list(found):
            found[p ^ bit] = lax.ppermute(found[p], axis, swap)
        bit //= 2
    return [found[p] for p in range(count)]


def weight_pieces(shard, axis):
    if shard.shape[0] % 16 == 0:
        return pieces_of(shard, axis), lax.axis_index(axis)
    return [lax.all_gather(shard, axis, axis=0, tiled=True)], jnp.int32(0)


def fetch(pieces, target, base, sems):
    copies = []
    for p, piece in enumerate(pieces):
        height = piece.shape[0]
        at = pl.multiple_of(jnp.bitwise_xor(base, p) * height, 16)
        copy = pltpu.make_async_copy(piece, target.at[pl.ds(at, height)], sems.at[p])
        copy.start()
        copies.append(copy)
    return copies


def project_kernel(count, base_ref, x_ref, cos_ref, sin_ref, *refs):
    pieces = refs[:count]
    w_ref, normed_ref, q_ref, kv_ref, gains_ref, sems = refs[count:]
    copies = fetch(pieces, w_ref, base_ref[0], sems)
    seqs, _, block, width = x_ref.shape
    rows = seqs * 2 * block
    x = x_ref[...].reshape(rows, width).astype(jnp.float32)
    scale = lax.rsqrt(jnp.mean(x * x, axis=1, keepdims=True) + EPSILON)
    scaled = x * scale
    for copy in copies:
        copy.wait()
    last = w_ref[:, w_ref.shape[1] - LANES :].astype(jnp.float32).T
    gains = last[HEAD : HEAD + 8, :]
    gains_ref[...] = gains
    normed = (scaled * gains[0:1, :]).astype(jnp.bfloat16)
    normed_ref[...] = normed
    cosine = jnp.concatenate([cos_ref[...]] * seqs, 0)
    sine = jnp.concatenate([sin_ref[...]] * seqs, 0)
    for t in range(0, w_ref.shape[1] // LANES):
        lo = t * LANES
        u = dot(normed, w_ref[:, lo : lo + LANES])
        if lo >= 2 * KV_WIDTH:
            at = lo - 2 * KV_WIDTH
            u = turn(u, cosine, sine).astype(jnp.bfloat16) * jnp.bfloat16(SCALE)
            q_ref[:, at : at + LANES] = u
        else:
            r = turn(u, cosine, sine)
            is_key = lane_ids(u.shape) + lo < KV_WIDTH
            kv_ref[:, lo : lo + LANES] = jnp.where(is_key, r, u).astype(jnp.bfloat16)


def project(base, inputs, cosine, sine, pieces):
    seqs, _, block, width = inputs.shape
    rows = seqs * 2 * block
    columns = pieces[0].shape[1]
    q_width = columns - 2 * KV_WIDTH
    return pl.pallas_call(
        functools.partial(project_kernel, len(pieces)),
        in_specs=[
            pl.BlockSpec(memory_space=pltpu.SMEM),
            pl.BlockSpec(memory_space=pltpu.VMEM),
            pl.BlockSpec(memory_space=pltpu.VMEM),
            pl.BlockSpec(memory_space=pltpu.VMEM),
        ]
        + [pl.BlockSpec(memory_space=pl.ANY)] * len(pieces),
        out_specs=[pl.BlockSpec(memory_space=pltpu.VMEM)] * 5,
        out_shape=[
            jax.ShapeDtypeStruct((width, columns), jnp.bfloat16),
            jax.ShapeDtypeStruct((rows, width), jnp.bfloat16),
            jax.ShapeDtypeStruct((rows, q_width), jnp.bfloat16),
            jax.ShapeDtypeStruct((rows, 2 * KV_WIDTH), jnp.bfloat16),
            jax.ShapeDtypeStruct((8, width), jnp.float32),
        ],
        scratch_shapes=[pltpu.SemaphoreType.DMA((len(pieces),))],
        compiler_params=pltpu.CompilerParams(vmem_limit_bytes=VMEM_BYTES),
        cost_estimate=pl.CostEstimate(
            flops=2 * rows * width * columns, bytes_accessed=8 * 1024 * 1024, transcendentals=0
        ),
        name="project",
    )(base, inputs, cosine, sine, *pieces)


def per_device(
    inputs, norm1_gain, q_weight, k_weight, v_weight, o_weight, norm2_gain,
    gate_weight, up_weight, down_weight, cotangent,
):
    seqs, _, block, width = inputs.shape
    rows = seqs * 2 * block
    ctx_count = lax.axis_size("ctx")
    ctx_rank = lax.axis_index("ctx")
    rank = ctx_rank.astype(jnp.int32).reshape(1)
    cosine, sine = rope_tables(ctx_rank, ctx_count, block)
    pad = 2 * HEAD - 2 * HEAD // 2
    packed = jnp.concatenate(
        [
            k_weight, v_weight, q_weight, norm1_gain[:, None], norm2_gain[:, None],
            jnp.zeros((q_weight.shape[0], pad - 2), jnp.bfloat16),
        ],
        1,
    )
    pieces, base = weight_pieces(packed, "wsh")
    base = base.astype(jnp.int32).reshape(1)
    w_all, normed, queries, kv_rows, gains = project(base, inputs, cosine, sine, pieces)
    gain_one, gain_two = gains[0:1], gains[1:2]
    queries = queries.reshape(seqs, 2, block, -1)
    pairs = lax.all_gather(
        kv_rows.reshape(seqs, 2, block, 2 * KV_WIDTH), "ctx", axis=2, tiled=True
    )
    weight_o = lax.all_gather(o_weight, "wsh", axis=0, tiled=True)
    weight_gate = lax.all_gather(gate_weight, "wsh", axis=0, tiled=True)
    weight_up = lax.all_gather(up_weight, "wsh", axis=0, tiled=True)
    weight_down = lax.all_gather(down_weight, "wsh", axis=0, tiled=True)
    attended, lse = attend(rank, queries, pairs, width)
    stream = inputs.reshape(rows, width).astype(jnp.float32)
    cot_rows = cotangent.reshape(rows, width)
    attn_rows = attended.reshape(rows, width).astype(jnp.bfloat16)
    middle = stream + dot(attn_rows, weight_o)
    scale_two = lax.rsqrt(jnp.mean(middle * middle, -1, keepdims=True) + EPSILON)
    normed_two = (middle * scale_two * gain_two).astype(jnp.bfloat16)
    gate_pre = dot(normed_two, weight_gate)
    up_pre = dot(normed_two, weight_up)
    gate_sig = jax.nn.sigmoid(gate_pre)
    gate_act = gate_pre * gate_sig
    hidden = (gate_act * up_pre).astype(jnp.bfloat16)
    output = (middle + dot(hidden, weight_down)).astype(jnp.bfloat16).reshape(inputs.shape)
    grad_down = dot(hidden, cot_rows, TN)
    grad_hidden = dot(cot_rows, weight_down, NT)
    grad_gate = (grad_hidden * up_pre * gate_sig * (1.0 + gate_pre * (1.0 - gate_sig))).astype(
        jnp.bfloat16
    )
    grad_up = (grad_hidden * gate_act).astype(jnp.bfloat16)
    grad_wgate = dot(normed_two, grad_gate, TN)
    grad_wup = dot(normed_two, grad_up, TN)
    grad_normed_two = dot(grad_gate, weight_gate, NT) + dot(grad_up, weight_up, NT)
    grad_gain_two = jnp.sum(grad_normed_two * middle * scale_two, 0)
    scaled_two = grad_normed_two * gain_two
    grad_middle = cot_rows.astype(jnp.float32) + scale_two * (
        scaled_two
        - middle * scale_two * scale_two * jnp.mean(scaled_two * middle, -1, keepdims=True)
    )

    def reduce_weight(grad):
        part = lax.psum_scatter(grad.astype(jnp.bfloat16), "wsh", scatter_dimension=0, tiled=True)
        return lax.psum(part, "ctx").astype(jnp.float32)

    grad_branch = grad_middle.astype(jnp.bfloat16)
    grad_wo = dot(attn_rows, grad_branch, TN)
    grad_attn = dot(grad_branch, weight_o, NT).astype(jnp.bfloat16)
    grad_q, grad_pairs = attend_back(
        rank, queries, pairs, grad_attn.reshape(seqs, 2, block, width), attended, lse, cosine, sine
    )
    grad_kv = lax.psum_scatter(grad_pairs, "ctx", scatter_dimension=2, tiled=True)
    grad_kv = grad_kv.reshape(seqs, 2 * block, 2 * KV_WIDTH).astype(jnp.float32)
    tile_cos = jnp.concatenate(
        [jnp.tile(cosine[:, :HEAD], (1, KV_HEADS)), jnp.ones((2 * block, KV_WIDTH))], 1
    )
    tile_sin = jnp.concatenate(
        [jnp.tile(-sine[:, :HEAD], (1, KV_HEADS)), jnp.zeros((2 * block, KV_WIDTH))], 1
    )
    lane = jnp.arange(2 * KV_WIDTH)
    partner = jnp.where(
        (lane & 32) == 0, jnp.roll(grad_kv, -32, -1), jnp.roll(grad_kv, 32, -1)
    )
    grad_kv = (grad_kv * tile_cos + partner * tile_sin).astype(jnp.bfloat16).reshape(rows, -1)
    grad_q = grad_q.reshape(rows, width)
    grad_wq = dot(normed, grad_q, TN)
    grad_wkv = dot(normed, grad_kv, TN)
    weight_kv = w_all[:, : 2 * KV_WIDTH]
    weight_q = w_all[:, 2 * KV_WIDTH : 2 * KV_WIDTH + width]
    grad_normed = dot(grad_q, weight_q, NT) + dot(grad_kv, weight_kv, NT)
    scale_one = lax.rsqrt(jnp.mean(stream * stream, -1, keepdims=True) + EPSILON)
    grad_gain_one = jnp.sum(grad_normed * stream * scale_one, 0)
    scaled_one = grad_normed * gain_one
    grad_stream = grad_middle + scale_one * (
        scaled_one
        - stream * scale_one * scale_one * jnp.mean(scaled_one * stream, -1, keepdims=True)
    )
    sum_kv = reduce_weight(grad_wkv)
    return (
        output,
        grad_stream.reshape(inputs.shape),
        reduce_weight(grad_gain_one),
        reduce_weight(grad_wq),
        sum_kv[:, :KV_WIDTH],
        sum_kv[:, KV_WIDTH:],
        reduce_weight(grad_wo),
        reduce_weight(grad_gain_two),
        reduce_weight(grad_wgate),
        reduce_weight(grad_wup),
        reduce_weight(grad_down),
    )


def solution(mesh):
    weight = P("wsh", None)
    rows = P("wsh", None, "ctx", None)
    gain = P("wsh")
    return jax.shard_map(
        per_device,
        mesh=mesh,
        in_specs=(
            rows, gain, weight, weight, weight, weight, gain, weight, weight, weight, rows,
        ),
        out_specs=(
            rows, rows, gain, weight, weight, weight, weight, gain, weight, weight, weight,
        ),
        check_vma=False,
    )
```

```python
import functools
import math

import jax
import jax.numpy as jnp
from jax import lax
from jax.experimental import pallas as pl
from jax.experimental.pallas import tpu as pltpu
from jax.sharding import PartitionSpec as P

HEADS = 15
KV_HEADS = 5
HEAD = 64
GROUPS = HEADS // KV_HEADS
KV_WIDTH = KV_HEADS * HEAD
LANES = 128
EPSILON = 1e-05
MASKED = -1e30
SCALE = HEAD ** (-0.5)
VMEM_BYTES = 56 * 1024 * 1024

NT = (((1,), (1,)), ((), ()))
TN = (((0,), (0,)), ((), ()))


def dot(a, b, dims=None):
    if dims is None:
        return jnp.dot(a, b, preferred_element_type=jnp.float32)
    return lax.dot_general(a, b, dims, preferred_element_type=jnp.float32)


def lane_ids(shape):
    return lax.broadcasted_iota(jnp.int32, shape, 1)


def turn(u, cosine, sine):
    first = (lane_ids(u.shape) & 32) == 0
    partner = jnp.where(first, pltpu.roll(u, 96, 1), pltpu.roll(u, 32, 1))
    return u * cosine + partner * sine


def rope_tables(ctx_rank, ctx_count, block_len):
    offsets = jnp.arange(block_len, dtype=jnp.int32)
    front = ctx_rank * block_len + offsets
    back = (2 * ctx_count - 1 - ctx_rank) * block_len + offsets
    places = jnp.concatenate([front, back]).astype(jnp.float32)
    half = HEAD // 2
    frequency = jnp.exp(jnp.arange(half).astype(jnp.float32) * (-math.log(10000.0) / half))
    angles = places[:, None] * frequency[None, :]
    cosine = jnp.cos(angles)
    sine = jnp.sin(angles)
    return (
        jnp.concatenate([cosine] * 4, 1),
        jnp.concatenate([-sine, sine, -sine, sine], 1),
    )


def load_tile(ref, lead, tile, width):
    lo = tile * LANES
    hi = min(lo + LANES, width)
    value = ref[lead + (slice(None), slice(lo, hi))].astype(jnp.float32)
    if hi - lo < LANES:
        value = jnp.concatenate(
            [value, jnp.zeros((value.shape[0], LANES - (hi - lo)), jnp.float32)], 1
        )
    return value


def place_head(value, parity_from, parity_to):
    if parity_from != parity_to:
        value = pltpu.roll(value, HEAD, 1)
    keep = (lane_ids(value.shape) // HEAD) == parity_to
    return jnp.where(keep, value, 0.0)


def head_rows(ref, half, head, parity, width):
    parts = []
    for g in range(GROUPS):
        j = head * GROUPS + g
        parts.append(place_head(load_tile(ref, (0, half), j // 2, width), j % 2, parity))
    return jnp.concatenate(parts, 0)


def fetch_pairs(n, block, seq, owners_ref, pieces, kv_ref, sems):
    if len(pieces) == 1:
        return [pltpu.make_async_copy(pieces[0].at[seq], kv_ref, sems.at[0])]
    side = n // 2
    copies = []
    for i, piece in enumerate(pieces):
        place = i if i < side else n + side - 1 - i if i < n - 1 else side
        rows = pl.ds(pl.multiple_of(owners_ref[place] * block, block), block)
        target = kv_ref.at[:, rows] if i < n - 1 else kv_ref.at[i - (n - 1), rows]
        copies.append(pltpu.make_async_copy(piece.at[seq], target, sems.at[i]))
    return copies


def attend_kernel(n, block, count, rank_ref, owners_ref, q_ref, *refs):
    o_ref, lse_ref, kv_ref, qs, wide, narrow, top, total, acc, sems = refs[count:]
    c = rank_ref[0]
    rows = GROUPS * block
    pair = 2 * block
    seq = pl.program_id(0)
    seqs = kv_ref.shape[0]

    @pl.when(seq == 0)
    def _():
        for b in range(seqs):
            for copy in fetch_pairs(n, block, b, owners_ref, refs[:count], kv_ref.at[b], sems.at[b]):
                copy.start()

    for b in range(seqs):

        @pl.when(seq == b)
        def _():
            for copy in fetch_pairs(n, block, b, owners_ref, refs[:count], kv_ref.at[b], sems.at[b]):
                copy.wait()

    q_at = lax.broadcasted_iota(jnp.int32, (rows, block), 0) % block
    k_at = lax.broadcasted_iota(jnp.int32, (rows, block), 1)
    causal = k_at <= q_at
    unroll = n if n <= 8 else 4
    for h in range(KV_HEADS):
        kt, kp = h // 2, h % 2
        vt, vp = (KV_HEADS + h) // 2, (KV_HEADS + h) % 2
        kl, vl = pl.ds(kt * LANES, LANES), pl.ds(vt * LANES, LANES)
        for half in range(2):
            qs[half] = head_rows(q_ref, half, h, kp, q_ref.shape[-1]).astype(jnp.bfloat16)
        top[...] = jnp.full_like(top, MASKED)

        def wide_scores(i, carry):
            s = dot(qs[1], kv_ref[seq, 0, pl.ds(i * pair, pair), kl], NT)
            wide[i] = s
            top[1] = jnp.maximum(top[1], jnp.maximum(s[:, :block], s[:, block:]))
            return carry

        lax.fori_loop(0, n // 2, wide_scores, 0, unroll=2)

        def narrow_scores(d, carry):
            sel = (d > c).astype(jnp.int32)
            s = dot(qs[sel], kv_ref[seq, sel, pl.ds(d * block, block), kl], NT)
            s = jnp.where(jnp.logical_or(causal, d != c), s, MASKED)
            narrow[d] = s
            top[sel] = jnp.maximum(top[sel], s)
            return carry

        lax.fori_loop(0, n, narrow_scores, 0, unroll=unroll)
        s = dot(qs[1], kv_ref[seq, 1, pl.ds(c * block, block), kl], NT)
        s = jnp.where(causal, s, MASKED)
        narrow[n] = s
        top[1] = jnp.maximum(top[1], s)
        for half in range(2):
            top[half] = jnp.broadcast_to(
                jnp.max(top[half], axis=1, keepdims=True), (rows, LANES)
            )
        total[...] = jnp.zeros_like(total)
        acc[...] = jnp.zeros_like(acc)

        def wide_sums(i, carry):
            t = top[1]
            s = wide[i]
            pa = jnp.exp(s[:, :block] - t)
            pb = jnp.exp(s[:, block:] - t)
            total[1] += pa + pb
            p = jnp.concatenate([pa, pb], 1).astype(jnp.bfloat16)
            acc[1] += dot(p, kv_ref[seq, 0, pl.ds(i * pair, pair), vl])
            return carry

        lax.fori_loop(0, n // 2, wide_sums, 0, unroll=2)

        def narrow_sums(d, carry):
            sel = (d > c).astype(jnp.int32)
            p = jnp.exp(narrow[d] - top[sel])
            total[sel] += p
            acc[sel] += dot(p.astype(jnp.bfloat16), kv_ref[seq, sel, pl.ds(d * block, block), vl])
            return carry

        lax.fori_loop(0, n, narrow_sums, 0, unroll=unroll)
        p = jnp.exp(narrow[n] - top[1])
        total[1] += p
        acc[1] += dot(p.astype(jnp.bfloat16), kv_ref[seq, 1, pl.ds(c * block, block), vl])
        for half in range(2):
            whole = jnp.broadcast_to(jnp.sum(total[half], axis=1, keepdims=True), (rows, LANES))
            out = acc[half] / whole
            lse = top[half] + jnp.log(whole)
            lse_ref[0, 2 * h + half : 2 * h + half + 1, :] = lse.T[0:1, :]
            for g in range(GROUPS):
                j = h * GROUPS + g
                value = out[g * block : (g + 1) * block]
                if vp != j % 2:
                    value = pltpu.roll(value, HEAD, 1)
                lo = j * HEAD
                o_ref[0, half, :, lo : lo + HEAD] = value[:, (j % 2) * HEAD : (j % 2 + 1) * HEAD]


def attend(rank, owners, queries, pieces, width):
    seqs, _, block, q_width = queries.shape
    n = owners.shape[0]
    rows = GROUPS * block
    count = len(pieces)
    here = lambda i: (i, 0, 0, 0)
    return pl.pallas_call(
        functools.partial(attend_kernel, n, block, count),
        grid=(seqs,),
        in_specs=[
            pl.BlockSpec(memory_space=pltpu.SMEM),
            pl.BlockSpec(memory_space=pltpu.SMEM),
            pl.BlockSpec((1, 2, block, q_width), here),
        ]
        + [pl.BlockSpec(memory_space=pl.ANY)] * count,
        out_specs=[
            pl.BlockSpec((1, 2, block, width), here),
            pl.BlockSpec((1, 2 * KV_HEADS, rows), lambda i: (i, 0, 0)),
        ],
        out_shape=[
            jax.ShapeDtypeStruct((seqs, 2, block, width), jnp.float32),
            jax.ShapeDtypeStruct((seqs, 2 * KV_HEADS, rows), jnp.float32),
        ],
        scratch_shapes=[
            pltpu.VMEM((seqs, 2, n * block, 2 * KV_WIDTH), jnp.bfloat16),
            pltpu.VMEM((2, rows, LANES), jnp.bfloat16),
            pltpu.VMEM((n // 2, rows, 2 * block), jnp.float32),
            pltpu.VMEM((n + 1, rows, block), jnp.float32),
            pltpu.VMEM((2, rows, LANES), jnp.float32),
            pltpu.VMEM((2, rows, LANES), jnp.float32),
            pltpu.VMEM((2, rows, LANES), jnp.float32),
            pltpu.SemaphoreType.DMA((seqs, count)),
        ],
        compiler_params=pltpu.CompilerParams(vmem_limit_bytes=VMEM_BYTES),
        cost_estimate=pl.CostEstimate(
            flops=4 * seqs * HEADS * block * block * HEAD * (2 * n + 1) * 8,
            bytes_accessed=4 * 1024 * 1024,
            transcendentals=HEADS * block * block * (2 * n + 1),
        ),
        name="attend",
    )(rank, owners, queries, *pieces)


def attend_back_kernel(
    n, block, count, seq, rank_ref, owners_ref, q_ref, do_ref, o_ref, lse_ref, cos_ref, sin_ref, *refs
):
    dq_ref, dkv_ref, kv_ref, qs, dos, inner, dqt, dkv, dq_full, sems = refs[count:]
    c = rank_ref[0]
    copies = fetch_pairs(n, block, seq, owners_ref, refs[:count], kv_ref.at[0], sems)
    for copy in copies:
        copy.start()
    for copy in copies:
        copy.wait()
    rows = GROUPS * block
    pair = 2 * block
    width = do_ref.shape[-1]
    k_at = lax.broadcasted_iota(jnp.int32, (block, rows), 0)
    q_at = lax.broadcasted_iota(jnp.int32, (block, rows), 1) % block
    causal = k_at <= q_at
    unroll = n if n <= 8 else 4
    dkv[...] = jnp.zeros_like(dkv)
    dq_full[...] = jnp.zeros_like(dq_full)
    for h in range(KV_HEADS):
        kt, kp = h // 2, h % 2
        vt, vp = (KV_HEADS + h) // 2, (KV_HEADS + h) % 2
        kl, vl = pl.ds(kt * LANES, LANES), pl.ds(vt * LANES, LANES)
        for half in range(2):
            qs[half] = head_rows(q_ref, half, h, kp, q_ref.shape[-1]).astype(jnp.bfloat16)
            inner_parts = []
            do_parts = []
            for g in range(GROUPS):
                j = h * GROUPS + g
                d_o = load_tile(do_ref, (0, half), j // 2, width)
                o = load_tile(o_ref, (0, half), j // 2, width)
                product = place_head(d_o * o, j % 2, j % 2)
                inner_parts.append(jnp.sum(product.T, axis=0, keepdims=True))
                do_parts.append(place_head(d_o, j % 2, vp))
            dos[half] = jnp.concatenate(do_parts, 0).astype(jnp.bfloat16)
            inner[half] = jnp.concatenate(inner_parts, 1)
        dqt[...] = jnp.zeros_like(dqt)

        def visit(sel, half, start, count, mask):
            keys = kv_ref[0, half, pl.ds(start, count), kl]
            values = kv_ref[0, half, pl.ds(start, count), vl]
            s = dot(keys, qs[sel], NT)
            p = jnp.exp(s - lse_ref[0, pl.ds(2 * h + sel, 1), :])
            if mask is not None:
                p = jnp.where(mask, p, 0.0)
            dp = dot(values, dos[sel], NT)
            ds = (p * (dp - inner[sel])).astype(jnp.bfloat16)
            dkv[half, pl.ds(start, count), kl] += dot(ds, qs[sel])
            dkv[half, pl.ds(start, count), vl] += dot(p.astype(jnp.bfloat16), dos[sel])
            dqt[sel] += dot(keys, ds, TN)

        def wide_visit(i, carry):
            visit(1, 0, i * pair, pair, None)
            return carry

        lax.fori_loop(0, n // 2, wide_visit, 0, unroll=2)

        def narrow_visit(d, carry):
            sel = (d > c).astype(jnp.int32)
            visit(sel, sel, d * block, block, jnp.logical_or(causal, d != c))
            return carry

        lax.fori_loop(0, n, narrow_visit, 0, unroll=unroll)
        visit(1, 1, c * block, block, causal)
        for half in range(2):
            grad = dqt[half].T * SCALE
            for g in range(GROUPS):
                j = h * GROUPS + g
                tile = pl.ds((j // 2) * LANES, LANES)
                dq_full[half, :, tile] += place_head(
                    grad[g * block : (g + 1) * block], kp, j % 2
                )
    for half in range(2):
        at = slice(half * block, (half + 1) * block)
        for t in range(dq_full.shape[-1] // LANES):
            value = turn(
                dq_full[half, :, t * LANES : (t + 1) * LANES], cos_ref[at], -sin_ref[at]
            ).astype(jnp.bfloat16)
            hi = min((t + 1) * LANES, width)
            dq_ref[0, half, :, t * LANES : hi] = value[:, : hi - t * LANES]
    for place in range(n):
        at = pl.multiple_of(owners_ref[place] * block, block)
        dkv_ref[place] = dkv[:, pl.ds(at, block), :].astype(jnp.bfloat16)


def attend_back(rank, owners, queries, pieces, seq, grad_attn, attended, lse, cosine, sine):
    _, _, block, q_width = queries.shape
    width = grad_attn.shape[-1]
    n = owners.shape[0]
    rows = GROUPS * block
    count = len(pieces)
    there = lambda i: (seq, 0, 0, 0)
    here = lambda i: (0, 0, 0, 0)
    return pl.pallas_call(
        functools.partial(attend_back_kernel, n, block, count, seq),
        grid=(1,),
        in_specs=[
            pl.BlockSpec(memory_space=pltpu.SMEM),
            pl.BlockSpec(memory_space=pltpu.SMEM),
            pl.BlockSpec((1, 2, block, q_width), there),
            pl.BlockSpec((1, 2, block, width), there),
            pl.BlockSpec((1, 2, block, width), there),
            pl.BlockSpec((1, 2 * KV_HEADS, rows), lambda i: (seq, 0, 0)),
            pl.BlockSpec((2 * block, LANES), lambda i: (0, 0)),
            pl.BlockSpec((2 * block, LANES), lambda i: (0, 0)),
        ]
        + [pl.BlockSpec(memory_space=pl.ANY)] * count,
        out_specs=[
            pl.BlockSpec((1, 2, block, width), here),
            pl.BlockSpec((n, 2, block, 2 * KV_WIDTH), here, pipeline_mode=pl.Buffered(1)),
        ],
        out_shape=[
            jax.ShapeDtypeStruct((1, 2, block, width), jnp.bfloat16),
            jax.ShapeDtypeStruct((n, 2, block, 2 * KV_WIDTH), jnp.bfloat16),
        ],
        scratch_shapes=[
            pltpu.VMEM((1, 2, n * block, 2 * KV_WIDTH), jnp.bfloat16),
            pltpu.VMEM((2, rows, LANES), jnp.bfloat16),
            pltpu.VMEM((2, rows, LANES), jnp.bfloat16),
            pltpu.VMEM((2, 1, rows), jnp.float32),
            pltpu.VMEM((2, LANES, rows), jnp.float32),
            pltpu.VMEM((2, n * block, 2 * KV_WIDTH), jnp.float32),
            pltpu.VMEM((2, block, q_width), jnp.float32),
            pltpu.SemaphoreType.DMA((count,)),
        ],
        compiler_params=pltpu.CompilerParams(vmem_limit_bytes=VMEM_BYTES),
        cost_estimate=pl.CostEstimate(
            flops=10 * HEADS * block * block * HEAD * (2 * n + 1) * 8,
            bytes_accessed=8 * 1024 * 1024,
            transcendentals=HEADS * block * block * (2 * n + 1),
        ),
        name="attend_back",
    )(rank, owners, queries, grad_attn, attended, lse, cosine, sine, *pieces)


def follow(value, *others):
    return lax.optimization_barrier((value,) + others)[0]


def swap_over(value, axis, bit):
    return lax.ppermute(value, axis, [(i, i ^ bit) for i in range(lax.axis_size(axis))])


def whole_weights(shard, dimension=0):
    return [lax.all_gather(shard, "wsh", axis=dimension, tiled=True)]


def near_pieces(shard, far):
    return [shard, swap_over(shard, "wsh", 1), far, swap_over(far, "wsh", 1)]


def fetch(pieces, target, base, sems):
    copies = []
    for p, piece in enumerate(pieces):
        height = piece.shape[0]
        at = pl.multiple_of(jnp.bitwise_xor(base, p) * height, 16)
        copy = pltpu.make_async_copy(piece, target.at[pl.ds(at, height)], sems.at[p])
        copy.start()
        copies.append(copy)
    return copies


def project_kernel(count, base_ref, x_ref, cos_ref, sin_ref, *refs):
    pieces = refs[:count]
    w_ref, normed_ref, q_ref, kv_ref, gains_ref, sems = refs[count:]
    copies = fetch(pieces, w_ref, base_ref[0], sems)
    seqs, _, block, width = x_ref.shape
    rows = seqs * 2 * block
    x = x_ref[...].reshape(rows, width).astype(jnp.float32)
    scale = lax.rsqrt(jnp.mean(x * x, axis=1, keepdims=True) + EPSILON)
    scaled = x * scale
    for copy in copies:
        copy.wait()
    last = w_ref[:, w_ref.shape[1] - LANES :].astype(jnp.float32).T
    gains = last[HEAD : HEAD + 8, :]
    gains_ref[...] = gains
    normed = (scaled * gains[0:1, :]).astype(jnp.bfloat16)
    normed_ref[...] = normed
    cosine = jnp.concatenate([cos_ref[...]] * seqs, 0)
    sine = jnp.concatenate([sin_ref[...]] * seqs, 0)
    for t in range(0, w_ref.shape[1] // LANES):
        lo = t * LANES
        u = dot(normed, w_ref[:, lo : lo + LANES])
        if lo >= 2 * KV_WIDTH:
            at = lo - 2 * KV_WIDTH
            u = turn(u, cosine, sine).astype(jnp.bfloat16) * jnp.bfloat16(SCALE)
            q_ref[:, at : at + LANES] = u
        else:
            r = turn(u, cosine, sine)
            is_key = lane_ids(u.shape) + lo < KV_WIDTH
            kv_ref[:, lo : lo + LANES] = jnp.where(is_key, r, u).astype(jnp.bfloat16)


def project(base, inputs, cosine, sine, pieces):
    seqs, _, block, width = inputs.shape
    rows = seqs * 2 * block
    columns = pieces[0].shape[1]
    q_width = columns - 2 * KV_WIDTH
    return pl.pallas_call(
        functools.partial(project_kernel, len(pieces)),
        in_specs=[
            pl.BlockSpec(memory_space=pltpu.SMEM),
            pl.BlockSpec(memory_space=pltpu.VMEM),
            pl.BlockSpec(memory_space=pltpu.VMEM),
            pl.BlockSpec(memory_space=pltpu.VMEM),
        ]
        + [pl.BlockSpec(memory_space=pl.ANY)] * len(pieces),
        out_specs=[pl.BlockSpec(memory_space=pltpu.VMEM)] * 5,
        out_shape=[
            jax.ShapeDtypeStruct((width, columns), jnp.bfloat16),
            jax.ShapeDtypeStruct((rows, width), jnp.bfloat16),
            jax.ShapeDtypeStruct((rows, q_width), jnp.bfloat16),
            jax.ShapeDtypeStruct((rows, 2 * KV_WIDTH), jnp.bfloat16),
            jax.ShapeDtypeStruct((8, width), jnp.float32),
        ],
        scratch_shapes=[pltpu.SemaphoreType.DMA((len(pieces),))],
        compiler_params=pltpu.CompilerParams(vmem_limit_bytes=VMEM_BYTES),
        cost_estimate=pl.CostEstimate(
            flops=2 * rows * width * columns, bytes_accessed=8 * 1024 * 1024, transcendentals=0
        ),
        name="project",
    )(base, inputs, cosine, sine, *pieces)


def padded_rows(height, count):
    return -(-height // 256) * 256 if count > 1 and height % 128 else height


def send_out(source, targets, base, sems, column=0):
    count = 1 if len(targets) == 1 else 4
    height, width = source.shape[0] // count, source.shape[1]
    rows = targets[0].shape[0]
    copies = []
    for p in range(count):
        target = targets[2] if p % 2 else targets[p // 2]
        row = rows if p == 3 else 0
        at = pl.multiple_of(jnp.bitwise_xor(base, p) * height, 16)
        copy = pltpu.make_async_copy(
            source.at[pl.ds(at, height)],
            target.at[pl.ds(row, height), pl.ds(column, width)],
            sems.at[p],
        )
        copy.start()
        copies.append(copy)
    return copies


def piece_shapes(height, width, count):
    rows = padded_rows(height // count, count)
    shapes = [rows] if count == 1 else [rows, rows, 2 * rows]
    return [jax.ShapeDtypeStruct((row, width), jnp.bfloat16) for row in shapes]


def as_column(row):
    return jnp.broadcast_to(row, (LANES, row.shape[1])).T


def feed_body(count, step, base_ref, x_ref, cot_ref, gains_ref, *refs):
    refs = list(refs)

    def take(k):
        got = refs[:k]
        del refs[:k]
        return got

    attended = take(1)[0]
    outs = 1 if count == 1 else 3
    o_in, gate_in, up_in, down_in = take(count), take(count), take(count), take(count)
    out_ref, middle_grad_ref, attn_grad_ref = take(3)
    gate_out, up_out = take(outs), take(outs)
    down_out = take(1) if count == 1 else up_out
    w_o, w_gate, w_up, w_down, g_o, g_gate, g_up, g_down = take(8)
    attn, middle, n2, n2t, cott, total, back, sems, down_sems = take(9)
    base = base_ref[0]
    copies_o = fetch(o_in, w_o, base, sems.at[0])
    copies_gate = fetch(gate_in, w_gate, base, sems.at[1])
    copies_up = fetch(up_in, w_up, base, sems.at[2])
    copies_down = []
    for p, piece in enumerate(down_in):
        part = piece.shape[1]
        at = pl.multiple_of(jnp.bitwise_xor(base, p) * part, LANES)
        copies_down.append(
            pltpu.make_async_copy(piece, w_down.at[:, pl.ds(at, part)], sems.at[3, p])
        )
        copies_down[-1].start()
    rows, width = attn.shape
    gain = gains_ref[1:2, :]
    attn[...] = attended[...].reshape(rows, width).astype(jnp.bfloat16)
    for copy in copies_o:
        copy.wait()
    mid = x_ref[...].reshape(rows, width).astype(jnp.float32) + dot(attn[...], w_o[...])
    middle[...] = mid
    scale = lax.rsqrt(jnp.mean(mid * mid, axis=1, keepdims=True) + EPSILON)
    normed = (mid * scale * gain).astype(jnp.bfloat16)
    n2[...] = normed
    n2t[...] = normed.T
    cott[...] = cot_ref[...].reshape(rows, width).T
    total[...] = jnp.zeros_like(total)
    back[...] = jnp.zeros_like(back)
    for copy in copies_gate + copies_up + copies_down:
        copy.wait()

    def chunk(f, carry):
        at = pl.multiple_of(f * step, step)
        cols = pl.ds(at, step)
        cot = cot_ref[...].reshape(rows, width)
        gate = dot(n2[...], w_gate[:, cols])
        up = dot(n2[...], w_up[:, cols])
        grad_hidden = dot(cot, w_down[:, cols])
        sig = jax.nn.sigmoid(gate)
        act = gate * sig
        hidden = (act * up).astype(jnp.bfloat16)
        grad_gate = (grad_hidden * up * (sig * (1.0 + gate * (1.0 - sig)))).astype(jnp.bfloat16)
        grad_up = (grad_hidden * act).astype(jnp.bfloat16)
        total[...] += dot(hidden, w_down[:, cols], NT)
        g_down[:, cols] = dot(cott[...], hidden).astype(jnp.bfloat16)
        g_gate[:, cols] = dot(n2t[...], grad_gate).astype(jnp.bfloat16)
        g_up[:, cols] = dot(n2t[...], grad_up).astype(jnp.bfloat16)
        back[...] += dot(grad_gate, w_gate[:, cols], NT) + dot(grad_up, w_up[:, cols], NT)
        return carry

    lax.fori_loop(0, w_gate.shape[1] // step, chunk, 0)
    copies = send_out(g_gate, gate_out, base, sems.at[1])
    copies += send_out(g_up, up_out, base, sems.at[2])
    if count == 1:
        copies += send_out(g_down, down_out, base, down_sems)
    else:
        part, height = g_down.shape[1] // count, width // count
        for p in range(count):
            target = up_out[2] if p % 2 else up_out[p // 2]
            row = up_out[0].shape[0] if p == 3 else 0
            at = pl.multiple_of(jnp.bitwise_xor(base, p) * part, LANES)
            for k in range(count):
                copy = pltpu.make_async_copy(
                    g_down.at[pl.ds(k * height, height), pl.ds(at, part)],
                    target.at[pl.ds(row, height), pl.ds(g_up.shape[1] + k * part, part)],
                    down_sems.at[p * count + k],
                )
                copy.start()
                copies.append(copy)
    mid = middle[...]
    scale = lax.rsqrt(jnp.mean(mid * mid, axis=1, keepdims=True) + EPSILON)
    out_ref[...] = (mid + total[...]).astype(jnp.bfloat16).reshape(out_ref.shape)
    grad = back[...]
    gain_grad = jnp.sum(grad * mid * scale, axis=0, keepdims=True)
    u = grad * gain
    grad_middle = cot_ref[...].reshape(rows, width).astype(jnp.float32) + scale * (
        u - mid * scale * scale * jnp.mean(u * mid, axis=1, keepdims=True)
    )
    middle_grad_ref[...] = grad_middle
    branch = grad_middle.astype(jnp.bfloat16)
    attn_grad_ref[...] = (
        dot(branch, w_o[...], NT).astype(jnp.bfloat16).reshape(attn_grad_ref.shape)
    )
    g_o[:, :width] = dot(attn[...], branch, TN).astype(jnp.bfloat16)
    column = as_column(gain_grad).astype(jnp.bfloat16)
    g_o[:, width:] = column[:, : g_o.shape[1] - width]
    copies += send_out(g_o, gate_out, base, sems.at[0], g_gate.shape[1])
    for copy in copies:
        copy.wait()


def feed(base, inputs, cotangent, gains, attended, o_in, gate_in, up_in, down_in):
    seqs, _, block, width = inputs.shape
    rows = seqs * 2 * block
    count = len(o_in)
    units = gate_in[0].shape[1]
    wide = width + HEAD
    outs = 1 if count == 1 else 3
    vmem = pl.BlockSpec(memory_space=pltpu.VMEM)
    hbm = pl.BlockSpec(memory_space=pl.ANY)
    bf, f32 = jnp.bfloat16, jnp.float32
    out = pl.pallas_call(
        functools.partial(feed_body, count, 256),
        in_specs=[pl.BlockSpec(memory_space=pltpu.SMEM)]
        + [vmem] * 4
        + [hbm] * (4 * count),
        out_specs=[vmem] * 3 + [hbm] * (3 if count == 1 else 6),
        out_shape=[
            jax.ShapeDtypeStruct(inputs.shape, bf),
            jax.ShapeDtypeStruct((rows, width), f32),
            jax.ShapeDtypeStruct(inputs.shape, bf),
        ]
        + piece_shapes(width, units + wide, count)
        + (
            piece_shapes(width, units, 1) * 2
            if count == 1
            else piece_shapes(width, 2 * units, count)
        ),
        scratch_shapes=[
            pltpu.VMEM((width, width), bf),
            pltpu.VMEM((width, units), bf),
            pltpu.VMEM((width, units), bf),
            pltpu.VMEM((width, units), bf),
            pltpu.VMEM((width, wide), bf),
            pltpu.VMEM((width, units), bf),
            pltpu.VMEM((width, units), bf),
            pltpu.VMEM((width, units), bf),
            pltpu.VMEM((rows, width), bf),
            pltpu.VMEM((rows, width), f32),
            pltpu.VMEM((rows, width), bf),
            pltpu.VMEM((width, rows), bf),
            pltpu.VMEM((width, rows), bf),
            pltpu.VMEM((rows, width), f32),
            pltpu.VMEM((rows, width), f32),
            pltpu.SemaphoreType.DMA((4, count)),
            pltpu.SemaphoreType.DMA((count * count,)),
        ],
        compiler_params=pltpu.CompilerParams(vmem_limit_bytes=VMEM_BYTES + 4 * 1024 * 1024),
        cost_estimate=pl.CostEstimate(
            flops=2 * rows * width * (9 * units + 3 * width),
            bytes_accessed=48 * 1024 * 1024,
            transcendentals=rows * units,
        ),
        name="feed",
    )(base, inputs, cotangent, gains, attended, *o_in, *gate_in, *up_in, *down_in)
    k = 3
    return out[0], out[1], out[2], out[k:]


def query_kernel(count, seqs, base_ref, normed_ref, w_ref, *refs):
    dq_in, part_ref, outs, g_q, sems = (
        refs[:seqs], refs[seqs], refs[seqs + 1 : -2], refs[-2], refs[-1],
    )
    rows, width = normed_ref.shape
    dq = jnp.concatenate([r[...].reshape(rows // seqs, width) for r in dq_in], 0)
    g_q[:, :width] = dot(normed_ref[...], dq, TN).astype(jnp.bfloat16)
    g_q[:, width:] = jnp.zeros((width, g_q.shape[1] - width), jnp.bfloat16)
    copies = send_out(g_q, outs, base_ref[0], sems)
    part_ref[...] = dot(dq, w_ref[:, 2 * KV_WIDTH : 2 * KV_WIDTH + width], NT)
    for copy in copies:
        copy.wait()


def query_grads(count, base, normed, w_all, grad_queries):
    rows, width = normed.shape
    seqs = len(grad_queries)
    vmem = pl.BlockSpec(memory_space=pltpu.VMEM)
    out = pl.pallas_call(
        functools.partial(query_kernel, count, seqs),
        in_specs=[pl.BlockSpec(memory_space=pltpu.SMEM)] + [vmem] * (2 + seqs),
        out_specs=[vmem] + [pl.BlockSpec(memory_space=pl.ANY)] * (1 if count == 1 else 3),
        out_shape=[jax.ShapeDtypeStruct((rows, width), jnp.float32)]
        + piece_shapes(width, width + HEAD, count),
        scratch_shapes=[
            pltpu.VMEM((width, width + HEAD), jnp.bfloat16),
            pltpu.SemaphoreType.DMA((count,)),
        ],
        compiler_params=pltpu.CompilerParams(vmem_limit_bytes=VMEM_BYTES),
        cost_estimate=pl.CostEstimate(
            flops=4 * rows * width * width, bytes_accessed=10 * 1024 * 1024, transcendentals=0
        ),
        name="query_grads",
    )(base, normed, w_all, *grad_queries)
    return out[0], out[1:]


def finish_kernel(
    count, seqs, base_ref, x_ref, normed_ref, w_ref, part_ref, middle_grad_ref, gains_ref,
    cos_ref, sin_ref, *refs,
):
    dkv_in, out_ref, outs, g_kv, sems = (
        refs[:seqs], refs[seqs], refs[seqs + 1 : -2], refs[-2], refs[-1],
    )
    rows, width = normed_ref.shape
    columns = 2 * KV_WIDTH
    dkv = jnp.concatenate([r[...].reshape(rows // seqs, columns) for r in dkv_in], 0)
    cosine = jnp.concatenate([cos_ref[...]] * seqs, 0)
    sine = -jnp.concatenate([sin_ref[...]] * seqs, 0)
    tiles = []
    for lo in range(0, columns, LANES):
        u = dkv[:, lo : lo + LANES]
        if lo < KV_WIDTH:
            u = jnp.where(lane_ids(u.shape) + lo < KV_WIDTH, turn(u, cosine, sine), u)
        tiles.append(u.astype(jnp.bfloat16))
    dkv = jnp.concatenate(tiles, 1)
    x = x_ref[...].reshape(rows, width).astype(jnp.float32)
    scale = lax.rsqrt(jnp.mean(x * x, axis=1, keepdims=True) + EPSILON)
    grad = part_ref[...] + dot(dkv, w_ref[:, :columns], NT)
    g_kv[:, :columns] = dot(normed_ref[...], dkv, TN).astype(jnp.bfloat16)
    gain_grad = jnp.sum(grad * x * scale, axis=0, keepdims=True)
    g_kv[:, columns:] = as_column(gain_grad).astype(jnp.bfloat16)
    copies = send_out(g_kv, outs, base_ref[0], sems)
    u = grad * gains_ref[0:1, :]
    out_ref[...] = (
        middle_grad_ref[...]
        + scale * (u - x * scale * scale * jnp.mean(u * x, axis=1, keepdims=True))
    ).reshape(out_ref.shape)
    for copy in copies:
        copy.wait()


def finish(count, base, inputs, normed, w_all, part, middle_grad, gains, cosine, sine, grad_pairs):
    rows, width = normed.shape
    seqs = len(grad_pairs)
    vmem = pl.BlockSpec(memory_space=pltpu.VMEM)
    out = pl.pallas_call(
        functools.partial(finish_kernel, count, seqs),
        in_specs=[pl.BlockSpec(memory_space=pltpu.SMEM)] + [vmem] * (8 + seqs),
        out_specs=[vmem] + [pl.BlockSpec(memory_space=pl.ANY)] * (1 if count == 1 else 3),
        out_shape=[jax.ShapeDtypeStruct(inputs.shape, jnp.float32)]
        + piece_shapes(width, 2 * KV_WIDTH + LANES, count),
        scratch_shapes=[
            pltpu.VMEM((width, 2 * KV_WIDTH + LANES), jnp.bfloat16),
            pltpu.SemaphoreType.DMA((count,)),
        ],
        compiler_params=pltpu.CompilerParams(vmem_limit_bytes=VMEM_BYTES),
        cost_estimate=pl.CostEstimate(
            flops=8 * rows * width * KV_WIDTH, bytes_accessed=14 * 1024 * 1024, transcendentals=0
        ),
        name="finish",
    )(base, inputs, normed, w_all, part, middle_grad, gains, cosine, sine, *grad_pairs)
    return out[0], out[1:]


def added(*values):
    total = values[0].astype(jnp.float32)
    for value in values[1:]:
        total = total + value.astype(jnp.float32)
    return total.astype(jnp.bfloat16)


def core_sums(group):
    if len(group) == 1:
        return group
    kept, passed, sent = group
    rows = kept.shape[0]
    came = swap_over(sent, "wsh", 1)
    return [added(kept, came[:rows]), added(passed, came[rows:])]


def far_sums(group):
    return added(group[0], swap_over(group[1], "wsh", 2))


def rank_bits():
    count = lax.axis_size("ctx")
    return [1 << i for i in range(count.bit_length() - 1)]


def split_sums(mine):
    rank = lax.axis_index("ctx")
    bits = rank_bits()
    for bit in bits:
        half = mine.shape[0] // 2
        upper = ((rank & bit) != 0).astype(jnp.int32)
        sent = lax.dynamic_slice_in_dim(mine, (1 - upper) * half, half, 0)
        kept = lax.dynamic_slice_in_dim(mine, upper * half, half, 0)
        mine = added(kept, swap_over(sent, "ctx", bit))
    for bit in reversed(bits):
        upper = (rank & bit) != 0
        other = swap_over(mine, "ctx", bit)
        mine = jnp.concatenate([jnp.where(upper, other, mine), jnp.where(upper, mine, other)], 0)
    return mine


def whole_sums(mine):
    for bit in rank_bits():
        mine = added(mine, swap_over(mine, "ctx", bit))
    return mine


def plain_sums(grad, dimension=0):
    part = lax.psum_scatter(grad, "wsh", scatter_dimension=dimension, tiled=True)
    return lax.psum(part, "ctx")


def ring_order(n):
    return [0, 2, 4, 6, 7, 5, 3, 1] if n == 8 else list(range(n))


def ring_steps(n):
    order = ring_order(n)
    onward = [(order[i], order[(i + 1) % n]) for i in range(n)]
    return onward, [(b, a) for a, b in onward]


def ring_owners(n, rank):
    order = jnp.array(ring_order(n), jnp.int32)
    steps = jnp.arange(n, dtype=jnp.int32)
    place = jnp.sum(jnp.where(order == rank, steps, 0))
    hit = ((place + steps) % n)[:, None] == steps[None, :]
    return jnp.sum(jnp.where(hit, order[None, :], 0), -1).astype(jnp.int32)


def ring_gather(own, n, beside):
    onward, backward = ring_steps(n)
    ahead, behind = [own], [own]
    side = n // 2
    for step in range(1, side):
        one = lax.ppermute(behind[-1], "ctx", onward)
        two = lax.ppermute(ahead[-1], "ctx", backward)
        if step in beside:
            one, two, beside[step] = lax.optimization_barrier((one, two, beside[step]))
        else:
            one, two = lax.optimization_barrier((one, two))
        behind.append(one)
        ahead.append(two)
    one = lax.ppermute(behind[-1][:, 0], "ctx", onward)
    two = lax.ppermute(ahead[-1][:, 1], "ctx", backward)
    if side in beside:
        one, two, beside[side] = lax.optimization_barrier((one, two, beside[side]))
    return ahead + behind[1:] + [one, two]


def ring_sums(terms, n, beside):
    onward, backward = ring_steps(n)
    side = n // 2

    def term(k, half=None):
        if half is None:
            return jnp.stack([one[k] for one in terms])
        return jnp.stack([one[k, half] for one in terms])

    one = lax.ppermute(term(side, 0), "ctx", onward)
    two = lax.ppermute(term(side, 1), "ctx", backward)
    one, two = lax.optimization_barrier((one, two))
    up = jnp.stack([added(term(side - 1, 0), one), term(side - 1, 1)], 1)
    down = jnp.stack([term(n - side + 1, 0), added(term(n - side + 1, 1), two)], 1)
    for k in range(side - 1, 0, -1):
        up = lax.ppermute(up, "ctx", onward)
        down = lax.ppermute(down, "ctx", backward)
        if k in beside:
            up, down, beside[k] = lax.optimization_barrier((up, down, beside[k]))
        else:
            up, down = lax.optimization_barrier((up, down))
        if k > 1:
            up = added(up, term(k - 1))
            down = added(down, term(n - k + 1))
    return term(0).astype(jnp.float32) + up.astype(jnp.float32) + down.astype(jnp.float32)


def per_device(
    inputs, norm1_gain, q_weight, k_weight, v_weight, o_weight, norm2_gain,
    gate_weight, up_weight, down_weight, cotangent,
):
    seqs, _, block, width = inputs.shape
    rows = seqs * 2 * block
    n = lax.axis_size("ctx")
    ctx_rank = lax.axis_index("ctx")
    rank = ctx_rank.astype(jnp.int32).reshape(1)
    owners = ring_owners(n, ctx_rank)
    cosine, sine = rope_tables(ctx_rank, n, block)
    packed = jnp.concatenate(
        [
            k_weight, v_weight, q_weight, norm1_gain[:, None], norm2_gain[:, None],
            jnp.zeros((q_weight.shape[0], HEAD - 2), jnp.bfloat16),
        ],
        1,
    )
    split = packed.shape[0] % 16 == 0 and lax.axis_size("wsh") == 4
    ringed = n <= 8
    if split:
        pieces = near_pieces(packed, swap_over(packed, "wsh", 2))
    else:
        pieces = whole_weights(packed)
    count = len(pieces)
    base = lax.axis_index("wsh").astype(jnp.int32) if count > 1 else jnp.int32(0)
    base = base.reshape(1)
    w_all, normed, queries, kv_rows, gains = project(base, inputs, cosine, sine, pieces)
    queries = queries.reshape(seqs, 2, block, -1)
    beside = {}
    if split:
        far_o = swap_over(follow(o_weight, pieces[2]), "wsh", 2)
        kv_rows, far_o = lax.optimization_barrier((kv_rows, far_o))
        far_gate = swap_over(follow(gate_weight, far_o), "wsh", 2)
        far_up = swap_over(follow(up_weight, far_gate), "wsh", 2)
        far_down = swap_over(follow(down_weight.T, far_up), "wsh", 2)
        beside = {2: far_gate, 4: far_up}
    kv_rows = kv_rows.reshape(seqs, 2, block, 2 * KV_WIDTH)
    if ringed:
        pairs = ring_gather(kv_rows, n, beside)
    else:
        pairs = [lax.all_gather(kv_rows, "ctx", axis=2, tiled=True)]
    attended, lse = attend(rank, owners, queries, pairs, width)
    if split:
        attended, far_down = lax.optimization_barrier((attended, far_down))
        o_in = near_pieces(o_weight, far_o)
        gate_in = near_pieces(gate_weight, beside[2])
        up_in = near_pieces(up_weight, beside[4])
        down_in = near_pieces(down_weight.T, far_down)
    else:
        o_in, gate_in, up_in = [whole_weights(w) for w in (o_weight, gate_weight, up_weight)]
        down_in = whole_weights(down_weight.T, 1)
    output, middle_grad, attn_grad, groups = feed(
        base, inputs, cotangent, gains, attended, o_in, gate_in, up_in, down_in
    )
    units = gate_weight.shape[1]
    beside = {}
    if split:
        kept_b, pass_b = core_sums(groups[:3])
        kept_a, passed, sent = groups[3:]
        came = swap_over(sent, "wsh", 1)
        tall = kept_a.shape[0]
        pass_up = added(passed[:, :units], came[tall:, :units])
        pass_down = added(passed[:, units:], came[tall:, units:])
        far_up = swap_over(pass_up, "wsh", 2)
        far_down = swap_over(follow(pass_down, far_up), "wsh", 2)
        far_b = swap_over(follow(pass_b, far_down), "wsh", 2)
        beside = {3: far_down, 1: far_b}
    grad_queries, terms = [], []
    for b in range(seqs):
        at = follow(rank, pass_up, pass_down, pass_b) if split and b else rank
        grad_q, term = attend_back(
            at, owners, queries, pairs, b, attn_grad, attended, lse, cosine, sine
        )
        grad_queries.append(grad_q)
        terms.append(term)
    if ringed:
        if split:
            terms[-1], far_up = lax.optimization_barrier((terms[-1], far_up))
        summed = list(ring_sums(terms, n, beside))
    else:
        summed = []
        for term in terms:
            ordered = jnp.zeros_like(term).at[owners].set(term)
            part = lax.psum_scatter(ordered, "ctx", scatter_dimension=0, tiled=False)
            summed.append(part.astype(jnp.float32))
    part, q_group = query_grads(count, base, normed, w_all, grad_queries)
    if split:
        mine = jnp.concatenate(
            [
                added(kept_a[:, :units], came[:tall, :units], far_up),
                added(kept_a[:, units:], came[:tall, units:], beside[3]),
            ],
            1,
        )
        sum_a = split_sums(mine).astype(jnp.float32)
        sum_q = far_sums(core_sums(q_group))
        sum_b = split_sums(jnp.concatenate([added(kept_b, beside[1]), sum_q], 1)).astype(jnp.float32)
        sum_gate, sum_q = sum_b, sum_b[:, units + width + HEAD :]
        sum_up = sum_a
        height = width // count
        per = units // count
        sum_down = jnp.concatenate(
            [sum_a[:height, units + k * per : units + (k + 1) * per] for k in range(count)], 0
        ).T
    else:
        sum_gate = plain_sums(groups[0]).astype(jnp.float32)
        sum_up = plain_sums(groups[1]).astype(jnp.float32)
        sum_down = plain_sums(groups[2], 1).astype(jnp.float32).T
        sum_q = plain_sums(q_group[0]).astype(jnp.float32)
    input_grad, kv_group = finish(
        count, base, inputs, normed, w_all, part, middle_grad, gains, cosine, sine, summed
    )
    if split:
        sum_kv = whole_sums(far_sums(core_sums(kv_group))).astype(jnp.float32)
    else:
        sum_kv = plain_sums(kv_group[0]).astype(jnp.float32)
    height = norm1_gain.shape[0]
    columns = 2 * KV_WIDTH
    return (
        output,
        input_grad,
        sum_kv[:height, columns],
        sum_q[:height, :width],
        sum_kv[:height, :KV_WIDTH],
        sum_kv[:height, KV_WIDTH:columns],
        sum_gate[:height, units : units + width],
        sum_gate[:height, units + width],
        sum_gate[:height, :units],
        sum_up[:height, :units],
        sum_down,
    )


def solution(mesh):
    weight = P("wsh", None)
    rows = P("wsh", None, "ctx", None)
    gain = P("wsh")
    return jax.shard_map(
        per_device,
        mesh=mesh,
        in_specs=(
            rows, gain, weight, weight, weight, weight, gain, weight, weight, weight, rows,
        ),
        out_specs=(
            rows, rows, gain, weight, weight, weight, weight, gain, weight, weight, weight,
        ),
        check_vma=False,
    )
```

```python
import functools
import math

import jax
import jax.numpy as jnp
from jax import lax
from jax.experimental import pallas as pl
from jax.experimental.pallas import tpu as pltpu
from jax.sharding import PartitionSpec as P

HEADS = 15
KV_HEADS = 5
HEAD = 64
GROUPS = HEADS // KV_HEADS
KV_WIDTH = KV_HEADS * HEAD
LANES = 128
EPSILON = 1e-05
MASKED = -1e30
SCALE = HEAD ** (-0.5)
VMEM_BYTES = 56 * 1024 * 1024

NT = (((1,), (1,)), ((), ()))
TN = (((0,), (0,)), ((), ()))


def dot(a, b, dims=None):
    if dims is None:
        return jnp.dot(a, b, preferred_element_type=jnp.float32)
    return lax.dot_general(a, b, dims, preferred_element_type=jnp.float32)


def lane_ids(shape):
    return lax.broadcasted_iota(jnp.int32, shape, 1)


def turn(u, cosine, sine):
    first = (lane_ids(u.shape) & 32) == 0
    partner = jnp.where(first, pltpu.roll(u, 96, 1), pltpu.roll(u, 32, 1))
    return u * cosine + partner * sine


def rope_tables(ctx_rank, ctx_count, block_len):
    offsets = jnp.arange(block_len, dtype=jnp.int32)
    front = ctx_rank * block_len + offsets
    back = (2 * ctx_count - 1 - ctx_rank) * block_len + offsets
    places = jnp.concatenate([front, back]).astype(jnp.float32)
    half = HEAD // 2
    frequency = jnp.exp(jnp.arange(half).astype(jnp.float32) * (-math.log(10000.0) / half))
    angles = places[:, None] * frequency[None, :]
    cosine = jnp.cos(angles)
    sine = jnp.sin(angles)
    return (
        jnp.concatenate([cosine] * 4, 1),
        jnp.concatenate([-sine, sine, -sine, sine], 1),
    )


def load_tile(ref, lead, tile, width):
    lo = tile * LANES
    hi = min(lo + LANES, width)
    value = ref[lead + (slice(None), slice(lo, hi))].astype(jnp.float32)
    if hi - lo < LANES:
        value = jnp.concatenate(
            [value, jnp.zeros((value.shape[0], LANES - (hi - lo)), jnp.float32)], 1
        )
    return value


def place_head(value, parity_from, parity_to):
    if parity_from != parity_to:
        value = pltpu.roll(value, HEAD, 1)
    keep = (lane_ids(value.shape) // HEAD) == parity_to
    return jnp.where(keep, value, 0.0)


def head_rows(ref, half, head, parity, width):
    parts = []
    for g in range(GROUPS):
        j = head * GROUPS + g
        parts.append(place_head(load_tile(ref, (0, half), j // 2, width), j % 2, parity))
    return jnp.concatenate(parts, 0)


def fetch_pairs(n, block, seq, owners_ref, pieces, kv_ref, sems):
    if len(pieces) == 1:
        return [pltpu.make_async_copy(pieces[0].at[seq], kv_ref, sems.at[0])]
    side = n // 2
    copies = []
    for i, piece in enumerate(pieces):
        place = i if i < side else n + side - 1 - i if i < n - 1 else side
        rows = pl.ds(pl.multiple_of(owners_ref[place] * block, block), block)
        target = kv_ref.at[:, rows] if i < n - 1 else kv_ref.at[i - (n - 1), rows]
        copies.append(pltpu.make_async_copy(piece.at[seq], target, sems.at[i]))
    return copies


def attend_kernel(n, block, count, rank_ref, owners_ref, q_ref, *refs):
    o_ref, lse_ref, kv_ref, qs, wide, narrow, top, total, acc, sems = refs[count:]
    c = rank_ref[0]
    rows = GROUPS * block
    pair = 2 * block
    seq = pl.program_id(0)
    seqs = kv_ref.shape[0]

    @pl.when(seq == 0)
    def _():
        for b in range(seqs):
            for copy in fetch_pairs(n, block, b, owners_ref, refs[:count], kv_ref.at[b], sems.at[b]):
                copy.start()

    for b in range(seqs):

        @pl.when(seq == b)
        def _():
            for copy in fetch_pairs(n, block, b, owners_ref, refs[:count], kv_ref.at[b], sems.at[b]):
                copy.wait()

    q_at = lax.broadcasted_iota(jnp.int32, (rows, block), 0) % block
    k_at = lax.broadcasted_iota(jnp.int32, (rows, block), 1)
    causal = k_at <= q_at
    unroll = n if n <= 8 else 4
    for h in range(KV_HEADS):
        kt, kp = h // 2, h % 2
        vt, vp = (KV_HEADS + h) // 2, (KV_HEADS + h) % 2
        kl, vl = pl.ds(kt * LANES, LANES), pl.ds(vt * LANES, LANES)
        for half in range(2):
            qs[half] = head_rows(q_ref, half, h, kp, q_ref.shape[-1]).astype(jnp.bfloat16)
        top[...] = jnp.full_like(top, MASKED)

        def wide_scores(i, carry):
            s = dot(qs[1], kv_ref[seq, 0, pl.ds(i * pair, pair), kl], NT)
            wide[i] = s
            top[1] = jnp.maximum(top[1], jnp.maximum(s[:, :block], s[:, block:]))
            return carry

        lax.fori_loop(0, n // 2, wide_scores, 0, unroll=2)

        def narrow_scores(d, carry):
            sel = (d > c).astype(jnp.int32)
            s = dot(qs[sel], kv_ref[seq, sel, pl.ds(d * block, block), kl], NT)
            s = jnp.where(jnp.logical_or(causal, d != c), s, MASKED)
            narrow[d] = s
            top[sel] = jnp.maximum(top[sel], s)
            return carry

        lax.fori_loop(0, n, narrow_scores, 0, unroll=unroll)
        s = dot(qs[1], kv_ref[seq, 1, pl.ds(c * block, block), kl], NT)
        s = jnp.where(causal, s, MASKED)
        narrow[n] = s
        top[1] = jnp.maximum(top[1], s)
        for half in range(2):
            top[half] = jnp.broadcast_to(
                jnp.max(top[half], axis=1, keepdims=True), (rows, LANES)
            )
        total[...] = jnp.zeros_like(total)
        acc[...] = jnp.zeros_like(acc)

        def wide_sums(i, carry):
            t = top[1]
            s = wide[i]
            pa = jnp.exp(s[:, :block] - t)
            pb = jnp.exp(s[:, block:] - t)
            total[1] += pa + pb
            p = jnp.concatenate([pa, pb], 1).astype(jnp.bfloat16)
            acc[1] += dot(p, kv_ref[seq, 0, pl.ds(i * pair, pair), vl])
            return carry

        lax.fori_loop(0, n // 2, wide_sums, 0, unroll=2)

        def narrow_sums(d, carry):
            sel = (d > c).astype(jnp.int32)
            p = jnp.exp(narrow[d] - top[sel])
            total[sel] += p
            acc[sel] += dot(p.astype(jnp.bfloat16), kv_ref[seq, sel, pl.ds(d * block, block), vl])
            return carry

        lax.fori_loop(0, n, narrow_sums, 0, unroll=unroll)
        p = jnp.exp(narrow[n] - top[1])
        total[1] += p
        acc[1] += dot(p.astype(jnp.bfloat16), kv_ref[seq, 1, pl.ds(c * block, block), vl])
        for half in range(2):
            whole = jnp.broadcast_to(jnp.sum(total[half], axis=1, keepdims=True), (rows, LANES))
            out = acc[half] / whole
            lse = top[half] + jnp.log(whole)
            lse_ref[0, 2 * h + half : 2 * h + half + 1, :] = lse.T[0:1, :]
            for g in range(GROUPS):
                j = h * GROUPS + g
                value = out[g * block : (g + 1) * block]
                if vp != j % 2:
                    value = pltpu.roll(value, HEAD, 1)
                lo = j * HEAD
                o_ref[0, half, :, lo : lo + HEAD] = value[:, (j % 2) * HEAD : (j % 2 + 1) * HEAD]


def attend(rank, owners, queries, pieces, width):
    seqs, _, block, q_width = queries.shape
    n = owners.shape[0]
    rows = GROUPS * block
    count = len(pieces)
    here = lambda i: (i, 0, 0, 0)
    return pl.pallas_call(
        functools.partial(attend_kernel, n, block, count),
        grid=(seqs,),
        in_specs=[
            pl.BlockSpec(memory_space=pltpu.SMEM),
            pl.BlockSpec(memory_space=pltpu.SMEM),
            pl.BlockSpec((1, 2, block, q_width), here),
        ]
        + [pl.BlockSpec(memory_space=pl.ANY)] * count,
        out_specs=[
            pl.BlockSpec((1, 2, block, width), here),
            pl.BlockSpec((1, 2 * KV_HEADS, rows), lambda i: (i, 0, 0)),
        ],
        out_shape=[
            jax.ShapeDtypeStruct((seqs, 2, block, width), jnp.float32),
            jax.ShapeDtypeStruct((seqs, 2 * KV_HEADS, rows), jnp.float32),
        ],
        scratch_shapes=[
            pltpu.VMEM((seqs, 2, n * block, 2 * KV_WIDTH), jnp.bfloat16),
            pltpu.VMEM((2, rows, LANES), jnp.bfloat16),
            pltpu.VMEM((n // 2, rows, 2 * block), jnp.float32),
            pltpu.VMEM((n + 1, rows, block), jnp.float32),
            pltpu.VMEM((2, rows, LANES), jnp.float32),
            pltpu.VMEM((2, rows, LANES), jnp.float32),
            pltpu.VMEM((2, rows, LANES), jnp.float32),
            pltpu.SemaphoreType.DMA((seqs, count)),
        ],
        compiler_params=pltpu.CompilerParams(vmem_limit_bytes=VMEM_BYTES),
        cost_estimate=pl.CostEstimate(
            flops=4 * seqs * HEADS * block * block * HEAD * (2 * n + 1) * 8,
            bytes_accessed=4 * 1024 * 1024,
            transcendentals=HEADS * block * block * (2 * n + 1),
        ),
        name="attend",
    )(rank, owners, queries, *pieces)


def attend_back_kernel(
    n, block, count, seq, rank_ref, owners_ref, q_ref, do_ref, o_ref, lse_ref, cos_ref, sin_ref, *refs
):
    dq_ref, dkv_ref, kv_ref, qs, dos, inner, dqt, dkv, dq_full, sems = refs[count:]
    c = rank_ref[0]
    copies = fetch_pairs(n, block, seq, owners_ref, refs[:count], kv_ref.at[0], sems)
    for copy in copies:
        copy.start()
    for copy in copies:
        copy.wait()
    rows = GROUPS * block
    pair = 2 * block
    width = do_ref.shape[-1]
    k_at = lax.broadcasted_iota(jnp.int32, (block, rows), 0)
    q_at = lax.broadcasted_iota(jnp.int32, (block, rows), 1) % block
    causal = k_at <= q_at
    unroll = n if n <= 8 else 4
    dkv[...] = jnp.zeros_like(dkv)
    dq_full[...] = jnp.zeros_like(dq_full)
    for h in range(KV_HEADS):
        kt, kp = h // 2, h % 2
        vt, vp = (KV_HEADS + h) // 2, (KV_HEADS + h) % 2
        kl, vl = pl.ds(kt * LANES, LANES), pl.ds(vt * LANES, LANES)
        for half in range(2):
            qs[half] = head_rows(q_ref, half, h, kp, q_ref.shape[-1]).astype(jnp.bfloat16)
            inner_parts = []
            do_parts = []
            for g in range(GROUPS):
                j = h * GROUPS + g
                d_o = load_tile(do_ref, (0, half), j // 2, width)
                o = load_tile(o_ref, (0, half), j // 2, width)
                product = place_head(d_o * o, j % 2, j % 2)
                inner_parts.append(jnp.sum(product.T, axis=0, keepdims=True))
                do_parts.append(place_head(d_o, j % 2, vp))
            dos[half] = jnp.concatenate(do_parts, 0).astype(jnp.bfloat16)
            inner[half] = jnp.concatenate(inner_parts, 1)
        dqt[...] = jnp.zeros_like(dqt)

        def visit(sel, half, start, count, mask):
            keys = kv_ref[0, half, pl.ds(start, count), kl]
            values = kv_ref[0, half, pl.ds(start, count), vl]
            s = dot(keys, qs[sel], NT)
            p = jnp.exp(s - lse_ref[0, pl.ds(2 * h + sel, 1), :])
            if mask is not None:
                p = jnp.where(mask, p, 0.0)
            dp = dot(values, dos[sel], NT)
            ds = (p * (dp - inner[sel])).astype(jnp.bfloat16)
            dkv[half, pl.ds(start, count), kl] += dot(ds, qs[sel])
            dkv[half, pl.ds(start, count), vl] += dot(p.astype(jnp.bfloat16), dos[sel])
            dqt[sel] += dot(keys, ds, TN)

        def wide_visit(i, carry):
            visit(1, 0, i * pair, pair, None)
            return carry

        lax.fori_loop(0, n // 2, wide_visit, 0, unroll=2)

        def narrow_visit(d, carry):
            sel = (d > c).astype(jnp.int32)
            visit(sel, sel, d * block, block, jnp.logical_or(causal, d != c))
            return carry

        lax.fori_loop(0, n, narrow_visit, 0, unroll=unroll)
        visit(1, 1, c * block, block, causal)
        for half in range(2):
            grad = dqt[half].T * SCALE
            for g in range(GROUPS):
                j = h * GROUPS + g
                tile = pl.ds((j // 2) * LANES, LANES)
                dq_full[half, :, tile] += place_head(
                    grad[g * block : (g + 1) * block], kp, j % 2
                )
    for half in range(2):
        at = slice(half * block, (half + 1) * block)
        for t in range(dq_full.shape[-1] // LANES):
            value = turn(
                dq_full[half, :, t * LANES : (t + 1) * LANES], cos_ref[at], -sin_ref[at]
            ).astype(jnp.bfloat16)
            hi = min((t + 1) * LANES, width)
            dq_ref[0, half, :, t * LANES : hi] = value[:, : hi - t * LANES]
    for place in range(n):
        at = pl.multiple_of(owners_ref[place] * block, block)
        dkv_ref[place] = dkv[:, pl.ds(at, block), :].astype(jnp.bfloat16)


def attend_back(rank, owners, queries, pieces, seq, grad_attn, attended, lse, cosine, sine):
    _, _, block, q_width = queries.shape
    width = grad_attn.shape[-1]
    n = owners.shape[0]
    rows = GROUPS * block
    count = len(pieces)
    there = lambda i: (seq, 0, 0, 0)
    here = lambda i: (0, 0, 0, 0)
    return pl.pallas_call(
        functools.partial(attend_back_kernel, n, block, count, seq),
        grid=(1,),
        in_specs=[
            pl.BlockSpec(memory_space=pltpu.SMEM),
            pl.BlockSpec(memory_space=pltpu.SMEM),
            pl.BlockSpec((1, 2, block, q_width), there),
            pl.BlockSpec((1, 2, block, width), there),
            pl.BlockSpec((1, 2, block, width), there),
            pl.BlockSpec((1, 2 * KV_HEADS, rows), lambda i: (seq, 0, 0)),
            pl.BlockSpec((2 * block, LANES), lambda i: (0, 0)),
            pl.BlockSpec((2 * block, LANES), lambda i: (0, 0)),
        ]
        + [pl.BlockSpec(memory_space=pl.ANY)] * count,
        out_specs=[
            pl.BlockSpec((1, 2, block, width), here),
            pl.BlockSpec((n, 2, block, 2 * KV_WIDTH), here, pipeline_mode=pl.Buffered(1)),
        ],
        out_shape=[
            jax.ShapeDtypeStruct((1, 2, block, width), jnp.bfloat16),
            jax.ShapeDtypeStruct((n, 2, block, 2 * KV_WIDTH), jnp.bfloat16),
        ],
        scratch_shapes=[
            pltpu.VMEM((1, 2, n * block, 2 * KV_WIDTH), jnp.bfloat16),
            pltpu.VMEM((2, rows, LANES), jnp.bfloat16),
            pltpu.VMEM((2, rows, LANES), jnp.bfloat16),
            pltpu.VMEM((2, 1, rows), jnp.float32),
            pltpu.VMEM((2, LANES, rows), jnp.float32),
            pltpu.VMEM((2, n * block, 2 * KV_WIDTH), jnp.float32),
            pltpu.VMEM((2, block, q_width), jnp.float32),
            pltpu.SemaphoreType.DMA((count,)),
        ],
        compiler_params=pltpu.CompilerParams(vmem_limit_bytes=VMEM_BYTES),
        cost_estimate=pl.CostEstimate(
            flops=10 * HEADS * block * block * HEAD * (2 * n + 1) * 8,
            bytes_accessed=8 * 1024 * 1024,
            transcendentals=HEADS * block * block * (2 * n + 1),
        ),
        name="attend_back",
    )(rank, owners, queries, grad_attn, attended, lse, cosine, sine, *pieces)


def follow(value, *others):
    return lax.optimization_barrier((value,) + others)[0]


def swap_over(value, axis, bit):
    return lax.ppermute(value, axis, [(i, i ^ bit) for i in range(lax.axis_size(axis))])


def whole_weights(shard, dimension=0):
    return [lax.all_gather(shard, "wsh", axis=dimension, tiled=True)]


def near_pieces(shard, far):
    return [shard, swap_over(shard, "wsh", 1), far, swap_over(far, "wsh", 1)]


def fetch(pieces, target, base, sems):
    copies = []
    for p, piece in enumerate(pieces):
        height = piece.shape[0]
        at = pl.multiple_of(jnp.bitwise_xor(base, p) * height, 16)
        copy = pltpu.make_async_copy(piece, target.at[pl.ds(at, height)], sems.at[p])
        copy.start()
        copies.append(copy)
    return copies


def project_kernel(count, base_ref, x_ref, cos_ref, sin_ref, *refs):
    pieces = refs[:count]
    w_ref, normed_ref, q_ref, kv_ref, gains_ref, sems = refs[count:]
    copies = fetch(pieces, w_ref, base_ref[0], sems)
    seqs, _, block, width = x_ref.shape
    rows = seqs * 2 * block
    x = x_ref[...].reshape(rows, width).astype(jnp.float32)
    scale = lax.rsqrt(jnp.mean(x * x, axis=1, keepdims=True) + EPSILON)
    scaled = x * scale
    for copy in copies:
        copy.wait()
    last = w_ref[:, w_ref.shape[1] - LANES :].astype(jnp.float32).T
    gains = last[HEAD : HEAD + 8, :]
    gains_ref[...] = gains
    normed = (scaled * gains[0:1, :]).astype(jnp.bfloat16)
    normed_ref[...] = normed
    cosine = jnp.concatenate([cos_ref[...]] * seqs, 0)
    sine = jnp.concatenate([sin_ref[...]] * seqs, 0)
    for t in range(0, w_ref.shape[1] // LANES):
        lo = t * LANES
        u = dot(normed, w_ref[:, lo : lo + LANES])
        if lo >= 2 * KV_WIDTH:
            at = lo - 2 * KV_WIDTH
            u = turn(u, cosine, sine).astype(jnp.bfloat16) * jnp.bfloat16(SCALE)
            q_ref[:, at : at + LANES] = u
        else:
            r = turn(u, cosine, sine)
            is_key = lane_ids(u.shape) + lo < KV_WIDTH
            kv_ref[:, lo : lo + LANES] = jnp.where(is_key, r, u).astype(jnp.bfloat16)


def project(base, inputs, cosine, sine, pieces):
    seqs, _, block, width = inputs.shape
    rows = seqs * 2 * block
    columns = pieces[0].shape[1]
    q_width = columns - 2 * KV_WIDTH
    return pl.pallas_call(
        functools.partial(project_kernel, len(pieces)),
        in_specs=[
            pl.BlockSpec(memory_space=pltpu.SMEM),
            pl.BlockSpec(memory_space=pltpu.VMEM),
            pl.BlockSpec(memory_space=pltpu.VMEM),
            pl.BlockSpec(memory_space=pltpu.VMEM),
        ]
        + [pl.BlockSpec(memory_space=pl.ANY)] * len(pieces),
        out_specs=[pl.BlockSpec(memory_space=pltpu.VMEM)] * 5,
        out_shape=[
            jax.ShapeDtypeStruct((width, columns), jnp.bfloat16),
            jax.ShapeDtypeStruct((rows, width), jnp.bfloat16),
            jax.ShapeDtypeStruct((rows, q_width), jnp.bfloat16),
            jax.ShapeDtypeStruct((rows, 2 * KV_WIDTH), jnp.bfloat16),
            jax.ShapeDtypeStruct((8, width), jnp.float32),
        ],
        scratch_shapes=[pltpu.SemaphoreType.DMA((len(pieces),))],
        compiler_params=pltpu.CompilerParams(vmem_limit_bytes=VMEM_BYTES),
        cost_estimate=pl.CostEstimate(
            flops=2 * rows * width * columns, bytes_accessed=8 * 1024 * 1024, transcendentals=0
        ),
        name="project",
    )(base, inputs, cosine, sine, *pieces)


def padded_rows(height, count):
    return -(-height // 256) * 256 if count > 1 and height % 128 else height


def send_out(source, targets, base, sems, column=0):
    count = 1 if len(targets) == 1 else 4
    height, width = source.shape[0] // count, source.shape[1]
    rows = targets[0].shape[0]
    copies = []
    for p in range(count):
        target = targets[2] if p % 2 else targets[p // 2]
        row = rows if p == 3 else 0
        at = pl.multiple_of(jnp.bitwise_xor(base, p) * height, 16)
        copy = pltpu.make_async_copy(
            source.at[pl.ds(at, height)],
            target.at[pl.ds(row, height), pl.ds(column, width)],
            sems.at[p],
        )
        copy.start()
        copies.append(copy)
    return copies


def piece_shapes(height, width, count):
    rows = padded_rows(height // count, count)
    shapes = [rows] if count == 1 else [rows, rows, 2 * rows]
    return [jax.ShapeDtypeStruct((row, width), jnp.bfloat16) for row in shapes]


def as_column(row):
    return jnp.broadcast_to(row, (LANES, row.shape[1])).T


def feed_body(count, step, base_ref, x_ref, cot_ref, gains_ref, *refs):
    refs = list(refs)

    def take(k):
        got = refs[:k]
        del refs[:k]
        return got

    attended = take(1)[0]
    outs = 1 if count == 1 else 3
    o_in, gate_in, up_in, down_in = take(count), take(count), take(count), take(count)
    out_ref, middle_grad_ref, attn_grad_ref = take(3)
    gate_out, up_out = take(outs), take(outs)
    down_out = take(1) if count == 1 else up_out
    w_o, w_gate, w_up, w_down, g_o, g_gate, g_up, g_down = take(8)
    attn, middle, n2, n2t, cott, total, back, sems, down_sems = take(9)
    base = base_ref[0]
    copies_o = fetch(o_in, w_o, base, sems.at[0])
    copies_gate = fetch(gate_in, w_gate, base, sems.at[1])
    copies_up = fetch(up_in, w_up, base, sems.at[2])
    copies_down = []
    for p, piece in enumerate(down_in):
        part = piece.shape[1]
        at = pl.multiple_of(jnp.bitwise_xor(base, p) * part, LANES)
        copies_down.append(
            pltpu.make_async_copy(piece, w_down.at[:, pl.ds(at, part)], sems.at[3, p])
        )
        copies_down[-1].start()
    rows, width = attn.shape
    gain = gains_ref[1:2, :]
    attn[...] = attended[...].reshape(rows, width).astype(jnp.bfloat16)
    for copy in copies_o:
        copy.wait()
    mid = x_ref[...].reshape(rows, width).astype(jnp.float32) + dot(attn[...], w_o[...])
    middle[...] = mid
    scale = lax.rsqrt(jnp.mean(mid * mid, axis=1, keepdims=True) + EPSILON)
    normed = (mid * scale * gain).astype(jnp.bfloat16)
    n2[...] = normed
    n2t[...] = normed.T
    cott[...] = cot_ref[...].reshape(rows, width).T
    total[...] = jnp.zeros_like(total)
    back[...] = jnp.zeros_like(back)
    for copy in copies_gate + copies_up + copies_down:
        copy.wait()

    def chunk(f, carry):
        at = pl.multiple_of(f * step, step)
        cols = pl.ds(at, step)
        cot = cot_ref[...].reshape(rows, width)
        gate = dot(n2[...], w_gate[:, cols])
        up = dot(n2[...], w_up[:, cols])
        grad_hidden = dot(cot, w_down[:, cols])
        sig = jax.nn.sigmoid(gate)
        act = gate * sig
        hidden = (act * up).astype(jnp.bfloat16)
        grad_gate = (grad_hidden * up * (sig * (1.0 + gate * (1.0 - sig)))).astype(jnp.bfloat16)
        grad_up = (grad_hidden * act).astype(jnp.bfloat16)
        total[...] += dot(hidden, w_down[:, cols], NT)
        g_down[:, cols] = dot(cott[...], hidden).astype(jnp.bfloat16)
        g_gate[:, cols] = dot(n2t[...], grad_gate).astype(jnp.bfloat16)
        g_up[:, cols] = dot(n2t[...], grad_up).astype(jnp.bfloat16)
        back[...] += dot(grad_gate, w_gate[:, cols], NT) + dot(grad_up, w_up[:, cols], NT)
        return carry

    lax.fori_loop(0, w_gate.shape[1] // step, chunk, 0)
    copies = send_out(g_gate, gate_out, base, sems.at[1])
    copies += send_out(g_up, up_out, base, sems.at[2])
    if count == 1:
        copies += send_out(g_down, down_out, base, down_sems)
    else:
        part, height = g_down.shape[1] // count, width // count
        for p in range(count):
            target = up_out[2] if p % 2 else up_out[p // 2]
            row = up_out[0].shape[0] if p == 3 else 0
            at = pl.multiple_of(jnp.bitwise_xor(base, p) * part, LANES)
            for k in range(count):
                copy = pltpu.make_async_copy(
                    g_down.at[pl.ds(k * height, height), pl.ds(at, part)],
                    target.at[pl.ds(row, height), pl.ds(g_up.shape[1] + k * part, part)],
                    down_sems.at[p * count + k],
                )
                copy.start()
                copies.append(copy)
    mid = middle[...]
    scale = lax.rsqrt(jnp.mean(mid * mid, axis=1, keepdims=True) + EPSILON)
    out_ref[...] = (mid + total[...]).astype(jnp.bfloat16).reshape(out_ref.shape)
    grad = back[...]
    gain_grad = jnp.sum(grad * mid * scale, axis=0, keepdims=True)
    u = grad * gain
    grad_middle = cot_ref[...].reshape(rows, width).astype(jnp.float32) + scale * (
        u - mid * scale * scale * jnp.mean(u * mid, axis=1, keepdims=True)
    )
    middle_grad_ref[...] = grad_middle
    branch = grad_middle.astype(jnp.bfloat16)
    attn_grad_ref[...] = (
        dot(branch, w_o[...], NT).astype(jnp.bfloat16).reshape(attn_grad_ref.shape)
    )
    g_o[:, :width] = dot(attn[...], branch, TN).astype(jnp.bfloat16)
    column = as_column(gain_grad).astype(jnp.bfloat16)
    g_o[:, width:] = column[:, : g_o.shape[1] - width]
    copies += send_out(g_o, gate_out, base, sems.at[0], g_gate.shape[1])
    for copy in copies:
        copy.wait()


def feed(base, inputs, cotangent, gains, attended, o_in, gate_in, up_in, down_in):
    seqs, _, block, width = inputs.shape
    rows = seqs * 2 * block
    count = len(o_in)
    units = gate_in[0].shape[1]
    wide = width + HEAD
    outs = 1 if count == 1 else 3
    vmem = pl.BlockSpec(memory_space=pltpu.VMEM)
    hbm = pl.BlockSpec(memory_space=pl.ANY)
    bf, f32 = jnp.bfloat16, jnp.float32
    out = pl.pallas_call(
        functools.partial(feed_body, count, 256),
        in_specs=[pl.BlockSpec(memory_space=pltpu.SMEM)]
        + [vmem] * 4
        + [hbm] * (4 * count),
        out_specs=[vmem] * 3 + [hbm] * (3 if count == 1 else 6),
        out_shape=[
            jax.ShapeDtypeStruct(inputs.shape, bf),
            jax.ShapeDtypeStruct((rows, width), f32),
            jax.ShapeDtypeStruct(inputs.shape, bf),
        ]
        + piece_shapes(width, units + wide, count)
        + (
            piece_shapes(width, units, 1) * 2
            if count == 1
            else piece_shapes(width, 2 * units, count)
        ),
        scratch_shapes=[
            pltpu.VMEM((width, width), bf),
            pltpu.VMEM((width, units), bf),
            pltpu.VMEM((width, units), bf),
            pltpu.VMEM((width, units), bf),
            pltpu.VMEM((width, wide), bf),
            pltpu.VMEM((width, units), bf),
            pltpu.VMEM((width, units), bf),
            pltpu.VMEM((width, units), bf),
            pltpu.VMEM((rows, width), bf),
            pltpu.VMEM((rows, width), f32),
            pltpu.VMEM((rows, width), bf),
            pltpu.VMEM((width, rows), bf),
            pltpu.VMEM((width, rows), bf),
            pltpu.VMEM((rows, width), f32),
            pltpu.VMEM((rows, width), f32),
            pltpu.SemaphoreType.DMA((4, count)),
            pltpu.SemaphoreType.DMA((count * count,)),
        ],
        compiler_params=pltpu.CompilerParams(vmem_limit_bytes=VMEM_BYTES + 4 * 1024 * 1024),
        cost_estimate=pl.CostEstimate(
            flops=2 * rows * width * (9 * units + 3 * width),
            bytes_accessed=48 * 1024 * 1024,
            transcendentals=rows * units,
        ),
        name="feed",
    )(base, inputs, cotangent, gains, attended, *o_in, *gate_in, *up_in, *down_in)
    k = 3
    return out[0], out[1], out[2], out[k:]


def query_kernel(count, seqs, base_ref, normed_ref, w_ref, *refs):
    dq_in, part_ref, outs, g_q, sems = (
        refs[:seqs], refs[seqs], refs[seqs + 1 : -2], refs[-2], refs[-1],
    )
    rows, width = normed_ref.shape
    dq = jnp.concatenate([r[...].reshape(rows // seqs, width) for r in dq_in], 0)
    g_q[:, :width] = dot(normed_ref[...], dq, TN).astype(jnp.bfloat16)
    g_q[:, width:] = jnp.zeros((width, g_q.shape[1] - width), jnp.bfloat16)
    copies = send_out(g_q, outs, base_ref[0], sems)
    part_ref[...] = dot(dq, w_ref[:, 2 * KV_WIDTH : 2 * KV_WIDTH + width], NT)
    for copy in copies:
        copy.wait()


def query_grads(count, base, normed, w_all, grad_queries):
    rows, width = normed.shape
    seqs = len(grad_queries)
    vmem = pl.BlockSpec(memory_space=pltpu.VMEM)
    out = pl.pallas_call(
        functools.partial(query_kernel, count, seqs),
        in_specs=[pl.BlockSpec(memory_space=pltpu.SMEM)] + [vmem] * (2 + seqs),
        out_specs=[vmem] + [pl.BlockSpec(memory_space=pl.ANY)] * (1 if count == 1 else 3),
        out_shape=[jax.ShapeDtypeStruct((rows, width), jnp.float32)]
        + piece_shapes(width, width + HEAD, count),
        scratch_shapes=[
            pltpu.VMEM((width, width + HEAD), jnp.bfloat16),
            pltpu.SemaphoreType.DMA((count,)),
        ],
        compiler_params=pltpu.CompilerParams(vmem_limit_bytes=VMEM_BYTES),
        cost_estimate=pl.CostEstimate(
            flops=4 * rows * width * width, bytes_accessed=10 * 1024 * 1024, transcendentals=0
        ),
        name="query_grads",
    )(base, normed, w_all, *grad_queries)
    return out[0], out[1:]


def finish_kernel(
    count, seqs, base_ref, x_ref, normed_ref, w_ref, part_ref, middle_grad_ref, gains_ref,
    cos_ref, sin_ref, *refs,
):
    dkv_in, out_ref, outs, g_kv, sems = (
        refs[:seqs], refs[seqs], refs[seqs + 1 : -2], refs[-2], refs[-1],
    )
    rows, width = normed_ref.shape
    columns = 2 * KV_WIDTH
    dkv = jnp.concatenate([r[...].reshape(rows // seqs, columns) for r in dkv_in], 0)
    cosine = jnp.concatenate([cos_ref[...]] * seqs, 0)
    sine = -jnp.concatenate([sin_ref[...]] * seqs, 0)
    tiles = []
    for lo in range(0, columns, LANES):
        u = dkv[:, lo : lo + LANES]
        if lo < KV_WIDTH:
            u = jnp.where(lane_ids(u.shape) + lo < KV_WIDTH, turn(u, cosine, sine), u)
        tiles.append(u.astype(jnp.bfloat16))
    dkv = jnp.concatenate(tiles, 1)
    x = x_ref[...].reshape(rows, width).astype(jnp.float32)
    scale = lax.rsqrt(jnp.mean(x * x, axis=1, keepdims=True) + EPSILON)
    grad = part_ref[...] + dot(dkv, w_ref[:, :columns], NT)
    g_kv[:, :columns] = dot(normed_ref[...], dkv, TN).astype(jnp.bfloat16)
    gain_grad = jnp.sum(grad * x * scale, axis=0, keepdims=True)
    g_kv[:, columns:] = as_column(gain_grad).astype(jnp.bfloat16)
    copies = send_out(g_kv, outs, base_ref[0], sems)
    u = grad * gains_ref[0:1, :]
    out_ref[...] = (
        middle_grad_ref[...]
        + scale * (u - x * scale * scale * jnp.mean(u * x, axis=1, keepdims=True))
    ).reshape(out_ref.shape)
    for copy in copies:
        copy.wait()


def finish(count, base, inputs, normed, w_all, part, middle_grad, gains, cosine, sine, grad_pairs):
    rows, width = normed.shape
    seqs = len(grad_pairs)
    vmem = pl.BlockSpec(memory_space=pltpu.VMEM)
    out = pl.pallas_call(
        functools.partial(finish_kernel, count, seqs),
        in_specs=[pl.BlockSpec(memory_space=pltpu.SMEM)] + [vmem] * (8 + seqs),
        out_specs=[vmem] + [pl.BlockSpec(memory_space=pl.ANY)] * (1 if count == 1 else 3),
        out_shape=[jax.ShapeDtypeStruct(inputs.shape, jnp.float32)]
        + piece_shapes(width, 2 * KV_WIDTH + LANES, count),
        scratch_shapes=[
            pltpu.VMEM((width, 2 * KV_WIDTH + LANES), jnp.bfloat16),
            pltpu.SemaphoreType.DMA((count,)),
        ],
        compiler_params=pltpu.CompilerParams(vmem_limit_bytes=VMEM_BYTES),
        cost_estimate=pl.CostEstimate(
            flops=8 * rows * width * KV_WIDTH, bytes_accessed=14 * 1024 * 1024, transcendentals=0
        ),
        name="finish",
    )(base, inputs, normed, w_all, part, middle_grad, gains, cosine, sine, *grad_pairs)
    return out[0], out[1:]


def added(*values):
    total = values[0].astype(jnp.float32)
    for value in values[1:]:
        total = total + value.astype(jnp.float32)
    return total.astype(jnp.bfloat16)


def core_sums(group):
    if len(group) == 1:
        return group
    kept, passed, sent = group
    rows = kept.shape[0]
    came = swap_over(sent, "wsh", 1)
    return [added(kept, came[:rows]), added(passed, came[rows:])]


def far_sums(group):
    return added(group[0], swap_over(group[1], "wsh", 2))


def rank_bits():
    count = lax.axis_size("ctx")
    return [1 << i for i in range(count.bit_length() - 1)]


def split_sums(mine):
    rank = lax.axis_index("ctx")
    bits = rank_bits()
    for bit in bits:
        half = mine.shape[0] // 2
        upper = ((rank & bit) != 0).astype(jnp.int32)
        sent = lax.dynamic_slice_in_dim(mine, (1 - upper) * half, half, 0)
        kept = lax.dynamic_slice_in_dim(mine, upper * half, half, 0)
        mine = added(kept, swap_over(sent, "ctx", bit))
    for bit in reversed(bits):
        upper = (rank & bit) != 0
        other = swap_over(mine, "ctx", bit)
        mine = jnp.concatenate([jnp.where(upper, other, mine), jnp.where(upper, mine, other)], 0)
    return mine


def whole_sums(mine):
    for bit in rank_bits():
        mine = added(mine, swap_over(mine, "ctx", bit))
    return mine


def plain_sums(grad, dimension=0):
    part = lax.psum_scatter(grad, "wsh", scatter_dimension=dimension, tiled=True)
    return lax.psum(part, "ctx")


def ring_order(n):
    return [0, 2, 4, 6, 7, 5, 3, 1] if n == 8 else list(range(n))


def ring_steps(n):
    order = ring_order(n)
    onward = [(order[i], order[(i + 1) % n]) for i in range(n)]
    return onward, [(b, a) for a, b in onward]


def ring_owners(n, rank):
    order = jnp.array(ring_order(n), jnp.int32)
    steps = jnp.arange(n, dtype=jnp.int32)
    place = jnp.sum(jnp.where(order == rank, steps, 0))
    hit = ((place + steps) % n)[:, None] == steps[None, :]
    return jnp.sum(jnp.where(hit, order[None, :], 0), -1).astype(jnp.int32)


def ring_gather(own, n, beside):
    onward, backward = ring_steps(n)
    ahead, behind = [own], [own]
    side = n // 2
    for step in range(1, side):
        one = lax.ppermute(behind[-1], "ctx", onward)
        two = lax.ppermute(ahead[-1], "ctx", backward)
        if step in beside:
            one, two, beside[step] = lax.optimization_barrier((one, two, beside[step]))
        else:
            one, two = lax.optimization_barrier((one, two))
        behind.append(one)
        ahead.append(two)
    one = lax.ppermute(behind[-1][:, 0], "ctx", onward)
    two = lax.ppermute(ahead[-1][:, 1], "ctx", backward)
    if side in beside:
        one, two, beside[side] = lax.optimization_barrier((one, two, beside[side]))
    return ahead + behind[1:] + [one, two]


def ring_sums(terms, n, beside):
    onward, backward = ring_steps(n)
    side = n // 2

    def term(k, half=None):
        if half is None:
            return jnp.stack([one[k] for one in terms])
        return jnp.stack([one[k, half] for one in terms])

    one = lax.ppermute(term(side, 0), "ctx", onward)
    two = lax.ppermute(term(side, 1), "ctx", backward)
    one, two = lax.optimization_barrier((one, two))
    up = jnp.stack([added(term(side - 1, 0), one), term(side - 1, 1)], 1)
    down = jnp.stack([term(n - side + 1, 0), added(term(n - side + 1, 1), two)], 1)
    for k in range(side - 1, 0, -1):
        up = lax.ppermute(up, "ctx", onward)
        down = lax.ppermute(down, "ctx", backward)
        if k in beside:
            up, down, beside[k] = lax.optimization_barrier((up, down, beside[k]))
        else:
            up, down = lax.optimization_barrier((up, down))
        if k > 1:
            up = added(up, term(k - 1))
            down = added(down, term(n - k + 1))
    return term(0).astype(jnp.float32) + up.astype(jnp.float32) + down.astype(jnp.float32)


def per_device(
    inputs, norm1_gain, q_weight, k_weight, v_weight, o_weight, norm2_gain,
    gate_weight, up_weight, down_weight, cotangent,
):
    seqs, _, block, width = inputs.shape
    rows = seqs * 2 * block
    n = lax.axis_size("ctx")
    ctx_rank = lax.axis_index("ctx")
    rank = ctx_rank.astype(jnp.int32).reshape(1)
    owners = ring_owners(n, ctx_rank)
    cosine, sine = rope_tables(ctx_rank, n, block)
    packed = jnp.concatenate(
        [
            k_weight, v_weight, q_weight, norm1_gain[:, None], norm2_gain[:, None],
            jnp.zeros((q_weight.shape[0], HEAD - 2), jnp.bfloat16),
        ],
        1,
    )
    split = packed.shape[0] % 16 == 0 and lax.axis_size("wsh") == 4
    ringed = n <= 8
    if split:
        pieces = near_pieces(packed, swap_over(packed, "wsh", 2))
    else:
        pieces = whole_weights(packed)
    count = len(pieces)
    base = lax.axis_index("wsh").astype(jnp.int32) if count > 1 else jnp.int32(0)
    base = base.reshape(1)
    w_all, normed, queries, kv_rows, gains = project(base, inputs, cosine, sine, pieces)
    queries = queries.reshape(seqs, 2, block, -1)
    beside = {}
    if split:
        far_o = swap_over(follow(o_weight, pieces[2]), "wsh", 2)
        kv_rows, far_o = lax.optimization_barrier((kv_rows, far_o))
        far_gate = swap_over(follow(gate_weight, far_o), "wsh", 2)
        far_up = swap_over(follow(up_weight, far_gate), "wsh", 2)
        far_down = swap_over(follow(down_weight.T, far_up), "wsh", 2)
        beside = {2: far_gate, 4: far_up}
    kv_rows = kv_rows.reshape(seqs, 2, block, 2 * KV_WIDTH)
    if ringed:
        pairs = ring_gather(kv_rows, n, beside)
    else:
        pairs = [lax.all_gather(kv_rows, "ctx", axis=2, tiled=True)]
    attended, lse = attend(rank, owners, queries, pairs, width)
    if split:
        attended, far_down = lax.optimization_barrier((attended, far_down))
        o_in = near_pieces(o_weight, far_o)
        gate_in = near_pieces(gate_weight, beside[2])
        up_in = near_pieces(up_weight, beside[4])
        down_in = near_pieces(down_weight.T, far_down)
    else:
        o_in, gate_in, up_in = [whole_weights(w) for w in (o_weight, gate_weight, up_weight)]
        down_in = whole_weights(down_weight.T, 1)
    output, middle_grad, attn_grad, groups = feed(
        base, inputs, cotangent, gains, attended, o_in, gate_in, up_in, down_in
    )
    units = gate_weight.shape[1]
    beside = {}
    if split:
        kept_b, pass_b = core_sums(groups[:3])
        kept_a, passed, sent = groups[3:]
        came = swap_over(sent, "wsh", 1)
        tall = kept_a.shape[0]
        pass_up = added(passed[:, :units], came[tall:, :units])
        pass_down = added(passed[:, units:], came[tall:, units:])
        far_up = swap_over(pass_up, "wsh", 2)
        far_down = swap_over(follow(pass_down, far_up), "wsh", 2)
        far_b = swap_over(follow(pass_b, far_down), "wsh", 2)
        beside = {2: far_down}
    grad_queries, terms = [], []
    for b in range(seqs):
        at = follow(rank, pass_up, pass_down, pass_b) if split and b else rank
        grad_q, term = attend_back(
            at, owners, queries, pairs, b, attn_grad, attended, lse, cosine, sine
        )
        grad_queries.append(grad_q)
        terms.append(term)
    if ringed:
        if split:
            terms[-1], far_up = lax.optimization_barrier((terms[-1], far_up))
        summed = list(ring_sums(terms, n, beside))
    else:
        summed = []
        for term in terms:
            ordered = jnp.zeros_like(term).at[owners].set(term)
            part = lax.psum_scatter(ordered, "ctx", scatter_dimension=0, tiled=False)
            summed.append(part.astype(jnp.float32))
    part, q_group = query_grads(count, base, normed, w_all, grad_queries)
    if split:
        mine = jnp.concatenate(
            [
                added(kept_a[:, :units], came[:tall, :units], far_up),
                added(kept_a[:, units:], came[:tall, units:], beside[2]),
            ],
            1,
        )
        sum_a = split_sums(mine).astype(jnp.float32)
        mine_q = far_sums(core_sums(q_group))
        sum_gate = split_sums(added(kept_b, far_b)).astype(jnp.float32)
        sum_up = sum_a
        height = width // count
        per = units // count
        sum_down = jnp.concatenate(
            [sum_a[:height, units + k * per : units + (k + 1) * per] for k in range(count)], 0
        ).T
    else:
        sum_gate = plain_sums(groups[0]).astype(jnp.float32)
        sum_up = plain_sums(groups[1]).astype(jnp.float32)
        sum_down = plain_sums(groups[2], 1).astype(jnp.float32).T
        sum_q = plain_sums(q_group[0]).astype(jnp.float32)
    input_grad, kv_group = finish(
        count, base, inputs, normed, w_all, part, middle_grad, gains, cosine, sine, summed
    )
    if split:
        mine_kv = far_sums(core_sums(kv_group))
        sum_kv = split_sums(jnp.concatenate([mine_kv, mine_q], 1)).astype(jnp.float32)
        sum_q = sum_kv[:, mine_kv.shape[1] :]
    else:
        sum_kv = plain_sums(kv_group[0]).astype(jnp.float32)
    height = norm1_gain.shape[0]
    columns = 2 * KV_WIDTH
    return (
        output,
        input_grad,
        sum_kv[:height, columns],
        sum_q[:height, :width],
        sum_kv[:height, :KV_WIDTH],
        sum_kv[:height, KV_WIDTH:columns],
        sum_gate[:height, units : units + width],
        sum_gate[:height, units + width],
        sum_gate[:height, :units],
        sum_up[:height, :units],
        sum_down,
    )


def solution(mesh):
    weight = P("wsh", None)
    rows = P("wsh", None, "ctx", None)
    gain = P("wsh")
    return jax.shard_map(
        per_device,
        mesh=mesh,
        in_specs=(
            rows, gain, weight, weight, weight, weight, gain, weight, weight, weight, rows,
        ),
        out_specs=(
            rows, rows, gain, weight, weight, weight, weight, gain, weight, weight, weight,
        ),
        check_vma=False,
    )
```
